128 devices in a mesh: gx: 8 (over y_hi, z), gy: 4 (over y_lo, core), gz: 4 (over x).
Axes of the slice: x: 4, y: 4 (y_hi: 2, y_lo: 2; y = y_hi * 2 + y_lo), z: 4, core: 2. Of those that a mesh axis runs over, the one named last changes fastest.
Arguments:
- popul: float32 [8, 4, 4, 456, 1152], P('gx', 'gy', 'gz'), may hold values from 0.2 to 0.8
- codes: int32 [256], P(('gx', 'gy', 'gz')), may hold values from 1 to 4, as said below
- solid: int32 [8, 4, 4, 24, 1152], P('gx', 'gy', 'gz'), may hold values 0 or 1
Outputs:
- fields: float32 [8, 4, 4, 456, 1152], P('gx', 'gy', 'gz')
The draws below stay inside these ranges and needn't reach their ends.
Inputs may be any that keep to these rules, and one draw needn't show every extreme that they name: code // 2 - 1 is the change of device number (in the order gx, gy, gz, cyclic) that the block takes and code % 2 its place there; the codes put every block at exactly one home place; blocks moving to the next device take place 0 there, those moving to the previous one take place 1 there; between some two consecutive devices exactly 1 block move each way.
All inputs are finite; a program needn't handle non-finite values. No bound on the sum of `solid` on one device may be relied on, other than what follows from the above.
Results may differ from the reference program's by a relative error of at most 0.0001.
Values sent between devices are 32-bit elements; how exact they have to be, the bound alone decides.
A program may use at most 128 MiB of HBM per device.

```python
import jax
import jax.numpy as jnp

BS = 24
SLOTS = 2
MOVE = 1
STEPS = 2
N_GX = 8
N_GY = 4
N_GZ = 4
DEVICES = 128


def draw_codes(key, part):
    key = jax.random.fold_in(key, 11)
    first_key, second_key = jax.random.split(key)
    moves = jax.random.randint(first_key, (DEVICES,), 0, MOVE + 1).astype(jnp.int32)
    moves = moves.at[0].set(MOVE)
    before = jnp.roll(moves, 1)
    places = jnp.arange(SLOTS, dtype=jnp.int32)[None, :]
    going_up = places >= SLOTS - moves[:, None]
    going_down = places < before[:, None]
    code_up = 2 * SLOTS + places - (SLOTS - moves[:, None])
    code_down = SLOTS - before[:, None] + places
    base = jnp.where(going_up, code_up, jnp.where(going_down, code_down, SLOTS + places))
    scores = jax.random.randint(second_key, (DEVICES, SLOTS), 0, 1 << 20) * SLOTS + places
    order = jnp.argsort(scores, axis=1)
    return jnp.take_along_axis(base, order, axis=1).reshape(-1).astype(jnp.int32)


def plant(values, key, least, top_value):
    spot = [jax.random.randint(jax.random.fold_in(key, axis), (), 0, length) for axis, length in enumerate(values.shape)]
    widest = values.shape.index(max(values.shape))
    beside = spot[:widest] + [(spot[widest] + 1) % values.shape[widest]] + spot[widest + 1:]
    return values.at[tuple(spot)].set(least).at[tuple(beside)].set(top_value)


def level_of(own_key, dims, pieces, low, top_value):
    level = 1.0
    for axis_at, parts in pieces:
        heights = jax.random.uniform(jax.random.fold_in(jax.random.fold_in(own_key, 6), axis_at), (parts,), jnp.float32, low / len(pieces), top_value / len(pieces))
        level = level * jnp.repeat(jnp.exp(heights), dims[axis_at] // parts).reshape((-1,) + (1,) * (len(dims) - 1 - axis_at))
    return level


def setup_inputs(seed: int = 0) -> dict:
    arg_keys = jax.random.split(jax.random.key(seed), 4)
    popul = jnp.clip(0.2 + 0.6 * jax.random.uniform(arg_keys[0], (N_GX, N_GY, N_GZ, 19 * BS, BS * SLOTS * BS), jnp.float32) ** level_of(arg_keys[0], (N_GX, N_GY, N_GZ, 19 * BS, BS * SLOTS * BS), ((0, 8), (1, 4), (2, 4)), -0.2, 0.2), 0.2, 0.8)
    codes = draw_codes(jax.random.fold_in(arg_keys[3], 71), 0)
    solid = plant((jax.random.randint(arg_keys[2], (N_GX, N_GY, N_GZ, BS, BS * SLOTS * BS), 0, 4) < 1).astype(jnp.int32), jax.random.fold_in(arg_keys[2], 1), 0, 1)
    return dict(popul=popul, codes=codes, solid=solid)


VELS = [(0, 0, 0), (1, 0, 0), (-1, 0, 0), (0, 1, 0), (0, -1, 0), (0, 0, 1), (0, 0, -1),
        (1, 1, 0), (-1, -1, 0), (1, -1, 0), (-1, 1, 0), (1, 0, 1), (-1, 0, -1),
        (1, 0, -1), (-1, 0, 1), (0, 1, 1), (0, -1, -1), (0, 1, -1), (0, -1, 1)]
WEIGHTS = [1.0 / 3.0] + [1.0 / 18.0] * 6 + [1.0 / 36.0] * 12
OPPOSITE = [VELS.index((-a, -b, -c)) for (a, b, c) in VELS]
OMEGA = 1.25


def collide(f, solid_cells):
    rho = sum(f[i] for i in range(19))
    mom_x = sum(VELS[i][0] * f[i] for i in range(19) if VELS[i][0] != 0)
    mom_y = sum(VELS[i][1] * f[i] for i in range(19) if VELS[i][1] != 0)
    mom_z = sum(VELS[i][2] * f[i] for i in range(19) if VELS[i][2] != 0)
    vel_x = mom_x / rho
    vel_y = mom_y / rho
    vel_z = mom_z / rho
    speed = vel_x * vel_x + vel_y * vel_y + vel_z * vel_z
    posts = []
    for i in range(19):
        along = VELS[i][0] * vel_x + VELS[i][1] * vel_y + VELS[i][2] * vel_z
        equil = WEIGHTS[i] * rho * (1.0 + 3.0 * along + 4.5 * along * along - 1.5 * speed)
        posts.append(f[i] - OMEGA * (f[i] - equil))
    fluid = jnp.stack(posts)
    bounced = jnp.stack([f[o] for o in OPPOSITE])
    return jnp.where(solid_cells[None] == 1, bounced, fluid)


def reference(popul, codes, solid):
    total = N_GX * N_GY * N_GZ
    blocks = popul.reshape(N_GX, N_GY, N_GZ, 19, BS, BS, SLOTS, BS)
    blocks = blocks.transpose(0, 1, 2, 6, 3, 4, 5, 7).reshape(total * SLOTS, 19, BS, BS, BS)
    owner = jnp.arange(total * SLOTS, dtype=jnp.int32) // SLOTS
    target = ((owner + codes // SLOTS - 1) % total) * SLOTS + codes % SLOTS
    source = jnp.argsort(target).astype(jnp.int32)
    home = blocks[source].reshape(N_GX, N_GY, N_GZ, SLOTS, 19, BS, BS, BS)
    f = home.transpose(4, 0, 5, 1, 6, 2, 3, 7).reshape(19, N_GX * BS, N_GY * BS, N_GZ * SLOTS * BS)
    solid_grid = solid.reshape(N_GX, N_GY, N_GZ, BS, BS, SLOTS * BS)
    solid_grid = solid_grid.transpose(0, 3, 1, 4, 2, 5).reshape(N_GX * BS, N_GY * BS, N_GZ * SLOTS * BS)
    for step in range(STEPS):
        post = collide(f, solid_grid)
        f = jnp.stack([jnp.roll(post[i], VELS[i], (0, 1, 2)) for i in range(19)])
    result = f.reshape(19, N_GX, BS, N_GY, BS, N_GZ, SLOTS * BS)
    result = result.transpose(1, 3, 5, 0, 2, 4, 6)
    return result.reshape(N_GX, N_GY, N_GZ, 19 * BS, BS * SLOTS * BS)
```

```python
import functools

import jax
import jax.numpy as jnp
from jax import lax
from jax.experimental import pallas as pl
from jax.experimental.pallas import tpu as pltpu
from jax.sharding import PartitionSpec as P

STEPS = 2
VELS = [
    (0, 0, 0),
    (1, 0, 0),
    (-1, 0, 0),
    (0, 1, 0),
    (0, -1, 0),
    (0, 0, 1),
    (0, 0, -1),
    (1, 1, 0),
    (-1, -1, 0),
    (1, -1, 0),
    (-1, 1, 0),
    (1, 0, 1),
    (-1, 0, -1),
    (1, 0, -1),
    (-1, 0, 1),
    (0, 1, 1),
    (0, -1, -1),
    (0, 1, -1),
    (0, -1, 1),
]
WEIGHTS = [1.0 / 3.0] + [1.0 / 18.0] * 6 + [1.0 / 36.0] * 12
OPPOSITE = [VELS.index((-a, -b, -c)) for a, b, c in VELS]
OMEGA = 1.25
MESH = pl.DeviceIdType.MESH
DIRS = VELS[1:]
BS = 24
ROW = 2 * BS
LANES = BS * ROW
TILES = BS // 8
COLS = LANES // 128
PACKED = 9 * TILES + 2


def with_component(axis, sign):
    return [i for i, c in enumerate(VELS) if c[axis] == sign]


def place_of(delta):
    sx, sy, sz = (lax.axis_size(a) for a in ("gx", "gy", "gz"))
    x, y, z = (lax.axis_index(a) for a in ("gx", "gy", "gz"))
    total = sx * sy * sz
    p = lax.rem((x * sy + y) * sz + z + (delta + total), total)
    return (p // (sy * sz), lax.rem(p // sz, sy), lax.rem(p, sz))


def beside(c):
    place = []
    for axis, by in zip(("gx", "gy", "gz"), c):
        size = lax.axis_size(axis)
        place.append(lax.rem(lax.axis_index(axis) + (by + size), size))
    return tuple(place)


def collide(f, solid):
    rho = functools.reduce(lambda a, b: a + b, f)
    inv = 1.0 / rho
    vel = []
    for axis in range(3):
        plus = [f[i] for i in with_component(axis, 1)]
        minus = [f[i] for i in with_component(axis, -1)]
        vel.append((sum(plus[1:], plus[0]) - sum(minus[1:], minus[0])) * inv)
    speed = vel[0] * vel[0] + vel[1] * vel[1] + vel[2] * vel[2]
    base = 1.0 - 1.5 * speed
    bounce = solid == 1
    posts = [None] * 19
    weighted = {w: (OMEGA * w) * rho for w in set(WEIGHTS)}
    for i in range(19):
        if posts[i] is not None:
            continue
        o = OPPOSITE[i]
        w = weighted[WEIGHTS[i]]
        if i == o:
            posts[i] = jnp.where(bounce, f[i], (1.0 - OMEGA) * f[i] + w * base)
            continue
        along = None
        for axis in range(3):
            if VELS[i][axis] == 1:
                along = vel[axis] if along is None else along + vel[axis]
            elif VELS[i][axis] == -1:
                along = -vel[axis] if along is None else along - vel[axis]
        even = w * (base + 4.5 * (along * along))
        odd = (3.0 * w) * along
        posts[i] = jnp.where(bounce, f[o], (1.0 - OMEGA) * f[i] + (even + odd))
        posts[o] = jnp.where(bounce, f[i], (1.0 - OMEGA) * f[o] + (even - odd))
    return posts


def kernel(
    codes, popul, solid, fields,
    cells, home, post, send_up, send_down, got_up, got_down,
    faces_x, faces_y, faces_z, got_x, got_y, got_z, got_xy, got_xz, got_yz,
    load_sem, ring_send, ring_recv, halo_send, halo_recv,
):
    load = pltpu.make_async_copy(popul, cells, load_sem)
    load.start()
    following, previous = place_of(1), place_of(-1)
    partners = [following, previous] + [beside(c) for c in DIRS]
    barrier = pltpu.get_barrier_semaphore()
    for partner in partners:
        pl.semaphore_signal(barrier, inc=1, device_id=partner, device_id_type=MESH)

    lane = lax.broadcasted_iota(jnp.int32, (8, LANES), 1)
    z = lax.rem(lane, ROW)
    first = z < BS
    ordered = jnp.broadcast_to(codes[1], (8, LANES)) >= 3
    from_low = first & (jnp.broadcast_to(jnp.minimum(codes[0], codes[1]), (8, LANES)) == 1)
    from_high = jnp.logical_not(first) & (
        jnp.broadcast_to(jnp.maximum(codes[0], codes[1]), (8, LANES)) == 4
    )
    load.wait()

    def both_orders(i, t):
        a = cells[i, 8 * t : 8 * t + 8, :]
        w = jnp.where(first, pltpu.roll(a, LANES - BS, 1), pltpu.roll(a, BS, 1))
        normal = jnp.where(ordered, a, w)
        home[i, 8 * t : 8 * t + 8, :] = normal
        return normal, jnp.where(ordered, w, a)

    def pairs():
        for t in range(TILES):
            for k in range(9):
                yield 9 * t + k, (2 * k, t), (2 * k + 1, t)
        yield 9 * TILES, (18, 0), (18, 1)
        yield 9 * TILES + 1, (18, 2), None

    for row, one, two in pairs():
        normal_one, swapped_one = both_orders(*one)
        normal_two, swapped_two = (normal_one, swapped_one) if two is None else both_orders(*two)
        send_up[row] = jnp.where(first, swapped_one, normal_two)
        send_down[row] = jnp.where(first, normal_one, swapped_two)

    pl.semaphore_wait(barrier, len(partners))
    ring = []
    for way, (source, target, device) in enumerate(
        ((send_up, got_up, following), (send_down, got_down, previous))
    ):
        copy = pltpu.make_async_remote_copy(
            src_ref=source,
            dst_ref=target,
            send_sem=ring_send.at[way],
            recv_sem=ring_recv.at[way],
            device_id=device,
            device_id_type=MESH,
        )
        copy.start()
        ring.append(copy)
    for copy in ring:
        copy.wait()

    for row, one, two in pairs():
        low, high = got_up[row], got_down[row]
        i, t = one
        here = slice(8 * t, 8 * t + 8)
        own = jnp.where(from_low, low, home[i, here, :])
        home[i, here, :] = jnp.where(from_high, pltpu.roll(high, BS, 1), own)
        if two is not None:
            i, t = two
            here = slice(8 * t, 8 * t + 8)
            own = jnp.where(from_low, pltpu.roll(low, LANES - BS, 1), home[i, here, :])
            home[i, here, :] = jnp.where(from_high, high, own)

    row_at = lax.broadcasted_iota(jnp.int32, (BS, LANES), 0)
    lane_at = lax.broadcasted_iota(jnp.int32, (BS, LANES), 1)
    z_at = lax.rem(lane_at, ROW)
    for step in range(STEPS):

        def one_tile(n, carry):
            t, j = n // COLS, lax.rem(n, COLS)
            rows = pl.ds(pl.multiple_of(t * 8, 8), 8)
            cols = pl.ds(pl.multiple_of(j * 128, 128), 128)
            posts = collide([home[i, rows, cols] for i in range(19)], solid[rows, cols])
            for i in range(19):
                post[i, rows, cols] = posts[i]
            return carry

        lax.fori_loop(0, TILES * COLS, one_tile, 0)

        copies = []

        def send(c, source, target):
            n = DIRS.index(c)
            copy = pltpu.make_async_remote_copy(
                src_ref=source,
                dst_ref=target,
                send_sem=halo_send.at[step, n],
                recv_sem=halo_recv.at[step, n],
                device_id=beside(c),
                device_id_type=MESH,
            )
            copy.start()
            copies.append(copy)

        for side, sign in enumerate((1, -1)):
            out_z = ROW - 1 if sign == 1 else 0
            packed = None
            for k, i in enumerate(with_component(2, sign)):
                for t in range(TILES):
                    q = TILES * k + t
                    part = post[i, 8 * t : 8 * t + 8, :]
                    part = pltpu.roll(part, (-sign * q) % LANES, 1) if q else part
                    packed = part if packed is None else jnp.where(z == out_z - sign * q, part, packed)
            faces_z[step, side] = packed
            send((0, 0, sign), faces_z.at[step, side], got_z.at[step, side])
        for side, sign in enumerate((1, -1)):
            exit_x = BS - 1 if sign == 1 else 0
            for k, i in enumerate(with_component(0, sign)):
                faces_x[step, side, k : k + 1, :] = post[i, exit_x : exit_x + 1, :]
            send((sign, 0, 0), faces_x.at[step, side], got_x.at[step, side])
        for side, sign in enumerate((1, -1)):
            at = LANES - 128 if sign == 1 else 0
            for k, i in enumerate(with_component(1, sign)):
                faces_y[step, side, k] = post[i, :, at : at + 128]
            send((0, sign, 0), faces_y.at[step, side], got_y.at[step, side])
        for i in range(7, 19):
            cx, cy, cz = VELS[i]
            rows = slice(BS - 8, BS) if cx == 1 else slice(0, 8)
            cols = slice(LANES - 128, LANES) if cy == 1 else slice(0, 128)
            if cz == 0:
                send(VELS[i], post.at[i, rows, cols], got_xy.at[step, i - 7])
            elif cy == 0:
                send(VELS[i], post.at[i, rows, :], got_xz.at[step, i - 11])
            else:
                send(VELS[i], post.at[i, :, cols], got_yz.at[step, i - 15])
        for copy in copies:
            copy.wait()

        target = fields if step == STEPS - 1 else home
        for i in range(19):
            cx, cy, cz = VELS[i]
            v = post[i]
            out_z = ROW - 1 if cz == 1 else 0
            at_y = lane_at >= LANES - ROW if cy == 1 else lane_at < ROW
            at_x = row_at == (BS - 1 if cx == 1 else 0)
            at_z = z_at == out_z
            side_x, side_y, side_z = (0 if c == 1 else 1 for c in (cx, cy, cz))
            shift_z = -cz * ROW

            def widened(tile):
                rest = jnp.zeros((tile.shape[0], LANES - 128), jnp.float32)
                return jnp.concatenate([rest, tile] if cy == 1 else [tile, rest], axis=1)

            if cz:
                k = with_component(2, cz).index(i)
                packed = got_z[step, side_z]
                parts = [
                    pltpu.roll(packed, (cz * (TILES * k + t) + shift_z) % LANES, 1)
                    for t in range(TILES)
                ]
                v = jnp.where(at_z, jnp.concatenate(parts, axis=0), v)
            if cy:
                k = with_component(1, cy).index(i)
                inside = at_y & jnp.logical_not(at_z) if cz else at_y
                v = jnp.where(inside, widened(got_y[step, side_y, k]), v)
            if cy and cz:
                edge = pltpu.roll(widened(got_yz[step, i - 15]), shift_z % LANES, 1)
                slot_y = ((BS - 1 if cy == 1 else 0) - cz) % BS
                v = jnp.where(lane_at == slot_y * ROW + out_z, edge, v)
            if cx:
                k = with_component(0, cx).index(i)
                row = jnp.broadcast_to(got_x[step, side_x, k : k + 1, :], (BS, LANES))
                if cy:
                    r = 7 if cx == 1 else 0
                    edge = widened(got_xy[step, i - 7, r : r + 1, :])
                    row = jnp.where(at_y, jnp.broadcast_to(edge, (BS, LANES)), row)
                if cz:
                    r = 7 if cx == 1 else 0
                    edge = pltpu.roll(got_xz[step, i - 11], shift_z % LANES, 1)[r : r + 1, :]
                    row = jnp.where(at_z, jnp.broadcast_to(edge, (BS, LANES)), row)
                v = jnp.where(at_x, row, v)
            if cx:
                v = pltpu.roll(v, cx % BS, 0)
            if cy or cz:
                v = pltpu.roll(v, (cy * ROW + cz) % LANES, 1)
            target[i] = v


def per_device(popul, codes, solid):
    vmem = pl.BlockSpec(memory_space=pltpu.VMEM)
    fields = pl.pallas_call(
        kernel,
        out_shape=jax.ShapeDtypeStruct((19, BS, LANES), jnp.float32),
        in_specs=[
            pl.BlockSpec(memory_space=pltpu.SMEM),
            pl.BlockSpec(memory_space=pl.ANY),
            vmem,
        ],
        out_specs=vmem,
        scratch_shapes=[
            pltpu.VMEM((19, BS, LANES), jnp.float32),
            pltpu.VMEM((19, BS, LANES), jnp.float32),
            pltpu.VMEM((19, BS, LANES), jnp.float32),
            pltpu.VMEM((PACKED, 8, LANES), jnp.float32),
            pltpu.VMEM((PACKED, 8, LANES), jnp.float32),
            pltpu.VMEM((PACKED, 8, LANES), jnp.float32),
            pltpu.VMEM((PACKED, 8, LANES), jnp.float32),
            pltpu.VMEM((STEPS, 2, 8, LANES), jnp.float32),
            pltpu.VMEM((STEPS, 2, 5, BS, 128), jnp.float32),
            pltpu.VMEM((STEPS, 2, 8, LANES), jnp.float32),
            pltpu.VMEM((STEPS, 2, 8, LANES), jnp.float32),
            pltpu.VMEM((STEPS, 2, 5, BS, 128), jnp.float32),
            pltpu.VMEM((STEPS, 2, 8, LANES), jnp.float32),
            pltpu.VMEM((STEPS, 4, 8, 128), jnp.float32),
            pltpu.VMEM((STEPS, 4, 8, LANES), jnp.float32),
            pltpu.VMEM((STEPS, 4, BS, 128), jnp.float32),
            pltpu.SemaphoreType.DMA,
            pltpu.SemaphoreType.DMA((2,)),
            pltpu.SemaphoreType.DMA((2,)),
            pltpu.SemaphoreType.DMA((STEPS, 18)),
            pltpu.SemaphoreType.DMA((STEPS, 18)),
        ],
        compiler_params=pltpu.CompilerParams(
            collective_id=0, has_side_effects=True, vmem_limit_bytes=48 * 1024 * 1024
        ),
        cost_estimate=pl.CostEstimate(flops=14_000_000, bytes_accessed=4_500_000, transcendentals=0),
    )(codes, popul.reshape(19, BS, LANES), solid.reshape(BS, LANES))
    return fields.reshape(popul.shape)


def solution(mesh):
    placed = (
        P("gx", "gy", "gz", None, None),
        P(("gx", "gy", "gz")),
        P("gx", "gy", "gz", None, None),
    )
    return jax.shard_map(
        per_device,
        mesh=mesh,
        in_specs=placed,
        out_specs=P("gx", "gy", "gz", None, None),
        check_vma=False,
    )
```

```python
import functools

import jax
import jax.numpy as jnp
from jax import lax
from jax.experimental import pallas as pl
from jax.experimental.pallas import tpu as pltpu
from jax.sharding import PartitionSpec as P

STEPS = 2
VELS = [
    (0, 0, 0),
    (1, 0, 0),
    (-1, 0, 0),
    (0, 1, 0),
    (0, -1, 0),
    (0, 0, 1),
    (0, 0, -1),
    (1, 1, 0),
    (-1, -1, 0),
    (1, -1, 0),
    (-1, 1, 0),
    (1, 0, 1),
    (-1, 0, -1),
    (1, 0, -1),
    (-1, 0, 1),
    (0, 1, 1),
    (0, -1, -1),
    (0, 1, -1),
    (0, -1, 1),
]
WEIGHTS = [1.0 / 3.0] + [1.0 / 18.0] * 6 + [1.0 / 36.0] * 12
OPPOSITE = [VELS.index((-a, -b, -c)) for a, b, c in VELS]
OMEGA = 1.25
MESH = pl.DeviceIdType.MESH
DIRS = VELS[1:]
BS = 24
ROW = 2 * BS
LANES = BS * ROW
TILES = BS // 8
COLS = LANES // 128
THIRD = LANES // 3
PAD = 8
SPOT = {0: 0, 2: 8, 1: 16}
FIRST_ROW = {0: 2, 2: 11, 1: 20}
PACKED = 29


def with_component(axis, sign):
    return [i for i, c in enumerate(VELS) if c[axis] == sign]


def place_of(delta):
    sx, sy, sz = (lax.axis_size(a) for a in ("gx", "gy", "gz"))
    x, y, z = (lax.axis_index(a) for a in ("gx", "gy", "gz"))
    total = sx * sy * sz
    p = lax.rem((x * sy + y) * sz + z + (delta + total), total)
    return (p // (sy * sz), lax.rem(p // sz, sy), lax.rem(p, sz))


def beside(c):
    place = []
    for axis, by in zip(("gx", "gy", "gz"), c):
        size = lax.axis_size(axis)
        place.append(lax.rem(lax.axis_index(axis) + (by + size), size))
    return tuple(place)


def collide(f, solid):
    rho = functools.reduce(lambda a, b: a + b, f)
    inv = 1.0 / rho
    vel = []
    for axis in range(3):
        plus = [f[i] for i in with_component(axis, 1)]
        minus = [f[i] for i in with_component(axis, -1)]
        vel.append((sum(plus[1:], plus[0]) - sum(minus[1:], minus[0])) * inv)
    speed = vel[0] * vel[0] + vel[1] * vel[1] + vel[2] * vel[2]
    base = 1.0 - 1.5 * speed
    bounce = solid == 1
    posts = [None] * 19
    weighted = {w: (OMEGA * w) * rho for w in set(WEIGHTS)}
    for i in range(19):
        if posts[i] is not None:
            continue
        o = OPPOSITE[i]
        w = weighted[WEIGHTS[i]]
        if i == o:
            posts[i] = jnp.where(bounce, f[i], (1.0 - OMEGA) * f[i] + w * base)
            continue
        along = None
        for axis in range(3):
            if VELS[i][axis] == 1:
                along = vel[axis] if along is None else along + vel[axis]
            elif VELS[i][axis] == -1:
                along = -vel[axis] if along is None else along - vel[axis]
        even = w * (base + 4.5 * (along * along))
        odd = (3.0 * w) * along
        posts[i] = jnp.where(bounce, f[o], (1.0 - OMEGA) * f[i] + (even + odd))
        posts[o] = jnp.where(bounce, f[i], (1.0 - OMEGA) * f[o] + (even - odd))
    return posts


def kernel(
    held_codes, popul, held_solid, fields,
    codes, solid, cells, home, flow, post, send_up, send_down, got_up, got_down,
    out_x, out_y, out_z, out_yz, got_x, got_y, got_z, got_yz, got_xy, got_xz,
    load_sem, ring_send, ring_recv, halo_send, halo_recv,
):
    def rows_of(t):
        return slice(8 * t, 8 * t + 8)

    def padded(t, by=0):
        return slice(PAD + 8 * t + by, PAD + 8 * t + 8 + by)

    sources = [
        (held_codes, codes),
        (popul.at[18], cells.at[18]),
        (popul.at[0:18, rows_of(0)], cells.at[0:18, rows_of(0)]),
        (popul.at[0:18, rows_of(2)], cells.at[0:18, rows_of(2)]),
        (popul.at[0:18, rows_of(1)], cells.at[0:18, rows_of(1)]),
        (held_solid, solid),
    ]
    loads = [
        pltpu.make_async_copy(source, target, load_sem.at[n])
        for n, (source, target) in enumerate(sources)
    ]
    for load in loads:
        load.start()
    following, previous = place_of(1), place_of(-1)
    partners = [following, previous] + [beside(c) for c in DIRS]
    barrier = pltpu.get_barrier_semaphore()
    for partner in partners:
        pl.semaphore_signal(barrier, inc=1, device_id=partner, device_id_type=MESH)

    lane = lax.broadcasted_iota(jnp.int32, (8, LANES), 1)
    z = lax.rem(lane, ROW)
    z_third = z[:, :THIRD]
    first = z < BS
    loads[0].wait()
    low_code = jnp.minimum(codes[0], codes[1])
    high_code = jnp.maximum(codes[0], codes[1])
    ordered = jnp.broadcast_to(codes[1], (8, LANES)) >= 3
    from_low = first & (jnp.broadcast_to(low_code, (8, LANES)) == 1)
    from_high = jnp.logical_not(first) & (jnp.broadcast_to(high_code, (8, LANES)) == 4)

    def both_orders(i, t):
        a = cells[i, rows_of(t), :]
        w = jnp.where(first, pltpu.roll(a, LANES - BS, 1), pltpu.roll(a, BS, 1))
        normal = jnp.where(ordered, a, w)
        home[i, rows_of(t), :] = normal
        return normal, jnp.where(ordered, w, a)

    def pack(row, one, two):
        normal_one, swapped_one = both_orders(*one)
        normal_two, swapped_two = (normal_one, swapped_one) if two is None else both_orders(*two)
        send_up[row] = jnp.where(first, swapped_one, normal_two)
        send_down[row] = jnp.where(first, normal_one, swapped_two)

    def pack_tile(t):
        for k in range(9):
            pack(FIRST_ROW[t] + k, (2 * k, t), (2 * k + 1, t))

    ring = {}

    def send_ring(n, rows, planes):
        pair = []
        for way, (source, target, device) in enumerate(
            ((send_up, got_up, following), (send_down, got_down, previous))
        ):
            copy = pltpu.make_async_remote_copy(
                src_ref=source.at[rows, planes, :],
                dst_ref=target.at[rows, planes, :],
                send_sem=ring_send.at[way, n],
                recv_sem=ring_recv.at[way, n],
                device_id=device,
                device_id_type=MESH,
            )
            copy.start()
            pair.append(copy)
        ring[n] = pair

    def await_ring(n):
        for copy in ring[n]:
            copy.wait_recv()

    def unpack(row, one, two, planes=slice(0, 8)):
        low, high = got_up[row, planes, :], got_down[row, planes, :]
        i, t = one
        here = slice(8 * t + planes.start, 8 * t + planes.stop)
        own = jnp.where(from_low[planes], low, home[i, here, :])
        home[i, here, :] = jnp.where(from_high[planes], pltpu.roll(high, BS, 1), own)
        if two is not None:
            i, t = two
            here = slice(8 * t + planes.start, 8 * t + planes.stop)
            own = jnp.where(from_low[planes], pltpu.roll(low, LANES - BS, 1), home[i, here, :])
            home[i, here, :] = jnp.where(from_high[planes], high, own)

    def unpack_tile(t, planes=slice(0, 8)):
        for k in range(9):
            unpack(FIRST_ROW[t] + k, (2 * k, t), (2 * k + 1, t), planes)

    def collide_tile(step, t):
        source = home if step == 0 else flow

        def one_column(j, carry):
            cols = pl.ds(pl.multiple_of(j * 128, 128), 128)
            posts = collide([source[i, rows_of(t), cols] for i in range(19)], solid[rows_of(t), cols])
            for i in range(19):
                post[step, i, padded(t), cols] = posts[i]
            return carry

        lax.fori_loop(0, COLS, one_column, 0)

    started = {}

    def send(step, group, c, source, target):
        n = DIRS.index(c) + (18 if group == "inner" else 0)
        copy = pltpu.make_async_remote_copy(
            src_ref=source,
            dst_ref=target,
            send_sem=halo_send.at[step, n],
            recv_sem=halo_recv.at[step, n],
            device_id=beside(c),
            device_id_type=MESH,
        )
        copy.start()
        started.setdefault((step, group), []).append(copy)

    def await_halo(step, group):
        for copy in started[step, group]:
            copy.wait_recv()

    def send_x(step, sign):
        side = 0 if sign == 1 else 1
        exit_x = PAD + (BS - 1 if sign == 1 else 0)
        group = ("x", sign)
        for k, i in enumerate(with_component(0, sign)):
            out_x[step, side, k : k + 1, :] = post[step, i, exit_x : exit_x + 1, :]
        send(step, group, (sign, 0, 0), out_x.at[step, side], got_x.at[step, side])
        for k, i in enumerate(with_component(0, sign)):
            cx, cy, cz = VELS[i]
            if cy:
                cols = slice(LANES - 128, LANES) if cy == 1 else slice(0, 128)
                send(step, group, VELS[i], out_x.at[step, side, k : k + 1, cols], got_xy.at[step, i - 7])
            if cz:
                send(step, group, VELS[i], out_x.at[step, side, k : k + 1, :], got_xz.at[step, i - 11])

    def send_yz(step, group, tiles):
        at = 1 if group == "inner" else 0
        begin, end = SPOT[tiles[0]], SPOT[tiles[-1]] + 8
        for side, sign in enumerate((1, -1)):
            exit_z = ROW - 1 if sign == 1 else 0
            packed = None
            for n, t in enumerate(tiles):
                for k, i in enumerate(with_component(2, sign)):
                    q = 3 * (5 * n + k)
                    part = pltpu.roll(post[step, i, padded(t), :], (-sign * (ROW + q)) % LANES, 1)
                    for g in range(3):
                        piece = part[:, THIRD * g : THIRD * g + THIRD]
                        if g:
                            piece = pltpu.roll(piece, (-sign * g) % THIRD, 1)
                        if packed is None:
                            packed = piece
                        else:
                            packed = jnp.where(z_third == exit_z - sign * (q + g), piece, packed)
            out_z[step, at, side] = packed
            send(step, group, (0, 0, sign), out_z.at[step, at, side], got_z.at[step, at, side])
        for side, sign in enumerate((1, -1)):
            col = LANES - 128 if sign == 1 else 0
            for k, i in enumerate(with_component(1, sign)):
                for t in tiles:
                    out_y[step, at, side, k, SPOT[t] : SPOT[t] + 8, :] = post[
                        step, i, padded(t), col : col + 128
                    ]
            send(
                step,
                group,
                (0, sign, 0),
                out_y.at[step, at, side, :, begin:end, :],
                got_y.at[step, at, side, :, begin:end, :],
            )
        for i in range(15, 19):
            col = LANES - 128 if VELS[i][1] == 1 else 0
            for t in tiles:
                out_yz[step, at, i - 15, SPOT[t] : SPOT[t] + 8, :] = post[
                    step, i, padded(t), col : col + 128
                ]
            send(
                step,
                group,
                VELS[i],
                out_yz.at[step, at, i - 15, begin:end, :],
                got_yz.at[step, at, i - 15, begin:end, :],
            )

    def fill_yz(step, group, tiles):
        at = 1 if group == "inner" else 0
        tile_lane = lane[:, :128]
        for n, t in enumerate(tiles):
            spot = slice(SPOT[t], SPOT[t] + 8)
            for i in range(3, 19):
                cx, cy, cz = VELS[i]
                if cz:
                    exit_z = ROW - 1 if cz == 1 else 0
                    side = 0 if cz == 1 else 1
                    q = 3 * (5 * n + with_component(2, cz).index(i))
                    packed = got_z[step, at, side]
                    parts = [
                        pltpu.roll(packed, (cz * (q + g)) % THIRD, 1) if q + g else packed
                        for g in range(3)
                    ]
                    post[step, i, padded(t), :] = jnp.where(
                        z == exit_z, jnp.concatenate(parts, axis=1), post[step, i, padded(t), :]
                    )
                if cy:
                    side = 0 if cy == 1 else 1
                    col = LANES - 128 if cy == 1 else 0
                    cols = slice(col, col + 128)
                    leaves = tile_lane >= 128 - ROW if cy == 1 else tile_lane < ROW
                    if cz:
                        leaves = leaves & (z[:, cols] != exit_z)
                    k = with_component(1, cy).index(i)
                    post[step, i, padded(t), cols] = jnp.where(
                        leaves, got_y[step, at, side, k, spot, :], post[step, i, padded(t), cols]
                    )
                if cy and cz:
                    from_y = BS - 1 if cy == 1 else 0
                    slot = ((from_y - cz) % BS) * ROW + exit_z
                    source = from_y * ROW + exit_z
                    cols = slice(slot // 128 * 128, slot // 128 * 128 + 128)
                    edge = pltpu.roll(got_yz[step, at, i - 15, spot, :], (slot - source) % 128, 1)
                    post[step, i, padded(t), cols] = jnp.where(
                        tile_lane == slot % 128, edge, post[step, i, padded(t), cols]
                    )

    def fill_x(step, sign):
        side = 0 if sign == 1 else 1
        row_at = PAD - 1 if sign == 1 else PAD + BS
        one_lane = lane[0:1]
        for k, i in enumerate(with_component(0, sign)):
            cx, cy, cz = VELS[i]
            row = got_x[step, side, k : k + 1, :]
            if cz:
                exit_z = ROW - 1 if cz == 1 else 0
                edge = pltpu.roll(got_xz[step, i - 11], (-cz * ROW) % LANES, 1)
                row = jnp.where(z[0:1] == exit_z, edge, row)
            post[step, i, row_at : row_at + 1, :] = row
            if cy:
                col = LANES - 128 if cy == 1 else 0
                cols = slice(col, col + 128)
                leaves = one_lane[:, :128] >= 128 - ROW if cy == 1 else one_lane[:, :128] < ROW
                post[step, i, row_at : row_at + 1, cols] = jnp.where(
                    leaves, got_xy[step, i - 7], row[:, cols]
                )

    def stream(step, t, which=range(19)):
        target = fields if step == STEPS - 1 else flow
        for i in which:
            cx, cy, cz = VELS[i]
            v = post[step, i, padded(t, -cx), :]
            shift = (cy * ROW + cz) % LANES
            target[i, rows_of(t), :] = pltpu.roll(v, shift, 1) if shift else v

    loads[1].wait()
    pack(0, (18, 0), (18, 1))
    pack(1, (18, 2), None)
    loads[2].wait()
    pack_tile(0)
    pl.semaphore_wait(barrier, len(partners))
    send_ring(0, slice(0, FIRST_ROW[0] + 9), slice(0, 8))
    loads[3].wait()
    pack_tile(2)
    send_ring(1, slice(FIRST_ROW[2], FIRST_ROW[2] + 9), slice(0, 8))
    loads[4].wait()
    pack_tile(1)
    middle = slice(FIRST_ROW[1], FIRST_ROW[1] + 9)
    send_ring(2, middle, slice(0, 1))
    send_ring(3, middle, slice(7, 8))
    send_ring(4, middle, slice(1, 7))
    loads[5].wait()

    await_ring(0)
    unpack(0, (18, 0), (18, 1))
    unpack(1, (18, 2), None)
    unpack_tile(0)
    collide_tile(0, 0)
    send_x(0, -1)
    await_ring(1)
    unpack_tile(2)
    collide_tile(0, 2)
    send_x(0, 1)
    await_ring(2)
    await_ring(3)
    unpack_tile(1, slice(0, 1))
    unpack_tile(1, slice(7, 8))
    collide_tile(0, 1)
    send_yz(0, "outer", (0, 2, 1))
    await_halo(0, "outer")
    fill_yz(0, "outer", (0, 2, 1))
    await_halo(0, ("x", -1))
    fill_x(0, -1)
    stream(0, 2)
    collide_tile(1, 2)
    send_x(1, 1)
    stream(0, 0)

    await_ring(4)
    unpack_tile(1)
    collide_tile(0, 1)
    send_yz(0, "inner", (1,))

    await_halo(0, ("x", 1))
    fill_x(0, 1)
    for i in with_component(0, 1):
        cx, cy, cz = VELS[i]
        shift = (cy * ROW + cz) % LANES
        row = post[0, i, PAD - 1 : PAD, :]
        flow[i, 0:1, :] = pltpu.roll(row, shift, 1) if shift else row
    collide_tile(1, 0)
    send_x(1, -1)
    send_yz(1, "outer", (0, 2))

    await_halo(0, "inner")
    fill_yz(0, "inner", (1,))
    stream(0, 1)
    collide_tile(1, 1)
    send_yz(1, "inner", (1,))

    await_halo(1, "outer")
    fill_yz(1, "outer", (0, 2))
    await_halo(1, ("x", 1))
    fill_x(1, 1)
    stream(1, 0, [i for i in range(19) if VELS[i][0] != -1])
    await_halo(1, ("x", -1))
    fill_x(1, -1)
    stream(1, 2, [i for i in range(19) if VELS[i][0] != 1])
    await_halo(1, "inner")
    fill_yz(1, "inner", (1,))
    stream(1, 1)
    stream(1, 0, with_component(0, -1))
    stream(1, 2, with_component(0, 1))
    for copies in list(ring.values()) + list(started.values()):
        for copy in copies:
            copy.wait_send()


def per_device(popul, codes, solid):
    vmem = pl.BlockSpec(memory_space=pltpu.VMEM)
    fields = pl.pallas_call(
        kernel,
        out_shape=jax.ShapeDtypeStruct((19, BS, LANES), jnp.float32),
        in_specs=[pl.BlockSpec(memory_space=pltpu.HBM)] * 3,
        out_specs=vmem,
        scratch_shapes=[
            pltpu.SMEM((2,), jnp.int32),
            pltpu.VMEM((BS, LANES), jnp.int32),
            pltpu.VMEM((19, BS, LANES), jnp.float32),
            pltpu.VMEM((19, BS, LANES), jnp.float32),
            pltpu.VMEM((19, BS, LANES), jnp.float32),
            pltpu.VMEM((STEPS, 19, BS + 2 * PAD, LANES), jnp.float32),
        ]
        + [pltpu.VMEM((PACKED, 8, LANES), jnp.float32)] * 4
        + [
            pltpu.VMEM((STEPS, 2, 5, LANES), jnp.float32),
            pltpu.VMEM((STEPS, 2, 2, 5, BS, 128), jnp.float32),
            pltpu.VMEM((STEPS, 2, 2, 8, THIRD), jnp.float32),
            pltpu.VMEM((STEPS, 2, 4, BS, 128), jnp.float32),
        ]
        * 2
        + [
            pltpu.VMEM((STEPS, 4, 1, 128), jnp.float32),
            pltpu.VMEM((STEPS, 4, 1, LANES), jnp.float32),
            pltpu.SemaphoreType.DMA((6,)),
            pltpu.SemaphoreType.DMA((2, 5)),
            pltpu.SemaphoreType.DMA((2, 5)),
            pltpu.SemaphoreType.DMA((STEPS, 36)),
            pltpu.SemaphoreType.DMA((STEPS, 36)),
        ],
        compiler_params=pltpu.CompilerParams(
            collective_id=0, has_side_effects=True, vmem_limit_bytes=40 * 1024 * 1024
        ),
        cost_estimate=pl.CostEstimate(flops=14_000_000, bytes_accessed=4_500_000, transcendentals=0),
    )(codes, popul.reshape(19, BS, LANES), solid.reshape(BS, LANES))
    return fields.reshape(popul.shape)


def solution(mesh):
    placed = (
        P("gx", "gy", "gz", None, None),
        P(("gx", "gy", "gz")),
        P("gx", "gy", "gz", None, None),
    )
    return jax.shard_map(
        per_device,
        mesh=mesh,
        in_specs=placed,
        out_specs=P("gx", "gy", "gz", None, None),
        check_vma=False,
    )
```

```python
import functools

import jax
import jax.numpy as jnp
from jax import lax
from jax.experimental import pallas as pl
from jax.experimental.pallas import tpu as pltpu
from jax.sharding import PartitionSpec as P

STEPS = 2
VELS = [
    (0, 0, 0),
    (1, 0, 0),
    (-1, 0, 0),
    (0, 1, 0),
    (0, -1, 0),
    (0, 0, 1),
    (0, 0, -1),
    (1, 1, 0),
    (-1, -1, 0),
    (1, -1, 0),
    (-1, 1, 0),
    (1, 0, 1),
    (-1, 0, -1),
    (1, 0, -1),
    (-1, 0, 1),
    (0, 1, 1),
    (0, -1, -1),
    (0, 1, -1),
    (0, -1, 1),
]
WEIGHTS = [1.0 / 3.0] + [1.0 / 18.0] * 6 + [1.0 / 36.0] * 12
OPPOSITE = [VELS.index((-a, -b, -c)) for a, b, c in VELS]
OMEGA = 1.25
MESH = pl.DeviceIdType.MESH
DIRS = VELS[1:]
BS = 24
ROW = 2 * BS
LANES = BS * ROW
TILES = BS // 8
COLS = LANES // 128
THIRD = LANES // 3
PAD = 8
SPOT = {0: 0, 2: 8, 1: 16}
FIRST_ROW = {0: 2, 2: 11, 1: 20}
PACKED = 29


def with_component(axis, sign):
    return [i for i, c in enumerate(VELS) if c[axis] == sign]


def place_of(delta):
    sx, sy, sz = (lax.axis_size(a) for a in ("gx", "gy", "gz"))
    x, y, z = (lax.axis_index(a) for a in ("gx", "gy", "gz"))
    total = sx * sy * sz
    p = lax.rem((x * sy + y) * sz + z + (delta + total), total)
    return (p // (sy * sz), lax.rem(p // sz, sy), lax.rem(p, sz))


def beside(c):
    place = []
    for axis, by in zip(("gx", "gy", "gz"), c):
        size = lax.axis_size(axis)
        place.append(lax.rem(lax.axis_index(axis) + (by + size), size))
    return tuple(place)


def collide(f, solid):
    rho = functools.reduce(lambda a, b: a + b, f)
    inv = 1.0 / rho
    vel = []
    for axis in range(3):
        plus = [f[i] for i in with_component(axis, 1)]
        minus = [f[i] for i in with_component(axis, -1)]
        vel.append((sum(plus[1:], plus[0]) - sum(minus[1:], minus[0])) * inv)
    speed = vel[0] * vel[0] + vel[1] * vel[1] + vel[2] * vel[2]
    base = 1.0 - 1.5 * speed
    bounce = solid == 1
    posts = [None] * 19
    weighted = {w: (OMEGA * w) * rho for w in set(WEIGHTS)}
    for i in range(19):
        if posts[i] is not None:
            continue
        o = OPPOSITE[i]
        w = weighted[WEIGHTS[i]]
        if i == o:
            posts[i] = jnp.where(bounce, f[i], (1.0 - OMEGA) * f[i] + w * base)
            continue
        along = None
        for axis in range(3):
            if VELS[i][axis] == 1:
                along = vel[axis] if along is None else along + vel[axis]
            elif VELS[i][axis] == -1:
                along = -vel[axis] if along is None else along - vel[axis]
        even = w * (base + 4.5 * (along * along))
        odd = (3.0 * w) * along
        posts[i] = jnp.where(bounce, f[o], (1.0 - OMEGA) * f[i] + (even + odd))
        posts[o] = jnp.where(bounce, f[i], (1.0 - OMEGA) * f[o] + (even - odd))
    return posts


def kernel(
    held_codes, popul, held_solid, fields,
    codes, solid, cells, home, flow, post, send_up, send_down, got_up, got_down,
    out_x, out_y, out_z, out_yz, got_x, got_y, got_z, got_yz, got_xy, got_xz,
    load_sem, ring_send, ring_recv, halo_send, halo_recv,
):
    def rows_of(t):
        return slice(8 * t, 8 * t + 8)

    def padded(t, by=0):
        return slice(PAD + 8 * t + by, PAD + 8 * t + 8 + by)

    sources = [
        (held_codes, codes),
        (popul.at[18], cells.at[18]),
        (popul.at[0:18, rows_of(0)], cells.at[0:18, rows_of(0)]),
        (popul.at[0:18, rows_of(2)], cells.at[0:18, rows_of(2)]),
        (popul.at[0:18, rows_of(1)], cells.at[0:18, rows_of(1)]),
        (held_solid, solid),
    ]
    loads = [
        pltpu.make_async_copy(source, target, load_sem.at[n])
        for n, (source, target) in enumerate(sources)
    ]
    for load in loads:
        load.start()
    following, previous = place_of(1), place_of(-1)
    partners = [following, previous] + [beside(c) for c in DIRS]
    barrier = pltpu.get_barrier_semaphore()
    for partner in partners:
        pl.semaphore_signal(barrier, inc=1, device_id=partner, device_id_type=MESH)

    lane = lax.broadcasted_iota(jnp.int32, (8, LANES), 1)
    z = lax.rem(lane, ROW)
    z_third = z[:, :THIRD]
    first = z < BS
    loads[0].wait()
    low_code = jnp.minimum(codes[0], codes[1])
    high_code = jnp.maximum(codes[0], codes[1])
    ordered = jnp.broadcast_to(codes[1], (8, LANES)) >= 3
    from_low = first & (jnp.broadcast_to(low_code, (8, LANES)) == 1)
    from_high = jnp.logical_not(first) & (jnp.broadcast_to(high_code, (8, LANES)) == 4)

    def both_orders(i, t):
        a = cells[i, rows_of(t), :]
        w = jnp.where(first, pltpu.roll(a, LANES - BS, 1), pltpu.roll(a, BS, 1))
        normal = jnp.where(ordered, a, w)
        home[i, rows_of(t), :] = normal
        return normal, jnp.where(ordered, w, a)

    def pack(row, one, two):
        normal_one, swapped_one = both_orders(*one)
        normal_two, swapped_two = (normal_one, swapped_one) if two is None else both_orders(*two)
        send_up[row] = jnp.where(first, swapped_one, normal_two)
        send_down[row] = jnp.where(first, normal_one, swapped_two)

    def pack_tile(t):
        for k in range(9):
            pack(FIRST_ROW[t] + k, (2 * k, t), (2 * k + 1, t))

    ring = {}

    def send_ring(n, rows, planes):
        pair = []
        for way, (source, target, device) in enumerate(
            ((send_up, got_up, following), (send_down, got_down, previous))
        ):
            copy = pltpu.make_async_remote_copy(
                src_ref=source.at[rows, planes, :],
                dst_ref=target.at[rows, planes, :],
                send_sem=ring_send.at[way, n],
                recv_sem=ring_recv.at[way, n],
                device_id=device,
                device_id_type=MESH,
            )
            copy.start()
            pair.append(copy)
        ring[n] = pair

    def await_ring(n):
        for copy in ring[n]:
            copy.wait_recv()

    def unpack(row, one, two, planes=slice(0, 8)):
        low, high = got_up[row, planes, :], got_down[row, planes, :]
        i, t = one
        here = slice(8 * t + planes.start, 8 * t + planes.stop)
        own = jnp.where(from_low[planes], low, home[i, here, :])
        home[i, here, :] = jnp.where(from_high[planes], pltpu.roll(high, BS, 1), own)
        if two is not None:
            i, t = two
            here = slice(8 * t + planes.start, 8 * t + planes.stop)
            own = jnp.where(from_low[planes], pltpu.roll(low, LANES - BS, 1), home[i, here, :])
            home[i, here, :] = jnp.where(from_high[planes], high, own)

    def unpack_tile(t, planes=slice(0, 8)):
        for k in range(9):
            unpack(FIRST_ROW[t] + k, (2 * k, t), (2 * k + 1, t), planes)

    def collide_tile(step, t):
        source = home if step == 0 else flow

        def one_column(j, carry):
            cols = pl.ds(pl.multiple_of(j * 128, 128), 128)
            posts = collide([source[i, rows_of(t), cols] for i in range(19)], solid[rows_of(t), cols])
            for i in range(19):
                post[step, i, padded(t), cols] = posts[i]
            return carry

        lax.fori_loop(0, COLS, one_column, 0, unroll=True)

    started = {}

    def send(step, group, c, source, target):
        n = DIRS.index(c) + (18 if group == "inner" else 0)
        copy = pltpu.make_async_remote_copy(
            src_ref=source,
            dst_ref=target,
            send_sem=halo_send.at[step, n],
            recv_sem=halo_recv.at[step, n],
            device_id=beside(c),
            device_id_type=MESH,
        )
        copy.start()
        started.setdefault((step, group), []).append(copy)

    def await_halo(step, group):
        for copy in started[step, group]:
            copy.wait_recv()

    def send_x(step, sign):
        side = 0 if sign == 1 else 1
        exit_x = PAD + (BS - 1 if sign == 1 else 0)
        group = ("x", sign)
        for k, i in enumerate(with_component(0, sign)):
            out_x[step, side, k : k + 1, :] = post[step, i, exit_x : exit_x + 1, :]
        send(step, group, (sign, 0, 0), out_x.at[step, side], got_x.at[step, side])
        for k, i in enumerate(with_component(0, sign)):
            cx, cy, cz = VELS[i]
            if cy:
                cols = slice(LANES - 128, LANES) if cy == 1 else slice(0, 128)
                send(step, group, VELS[i], out_x.at[step, side, k : k + 1, cols], got_xy.at[step, i - 7])
            if cz:
                send(step, group, VELS[i], out_x.at[step, side, k : k + 1, :], got_xz.at[step, i - 11])

    def send_yz(step, group, tiles):
        at = 1 if group == "inner" else 0
        begin, end = SPOT[tiles[0]], SPOT[tiles[-1]] + 8
        for side, sign in enumerate((1, -1)):
            exit_z = ROW - 1 if sign == 1 else 0
            packed = None
            for n, t in enumerate(tiles):
                for k, i in enumerate(with_component(2, sign)):
                    q = 3 * (5 * n + k)
                    part = post[step, i, padded(t), :]
                    for g in range(3):
                        turned = pltpu.roll(part, (-sign * (ROW + q + g)) % LANES, 1)
                        piece = turned[:, THIRD * g : THIRD * g + THIRD]
                        if packed is None:
                            packed = piece
                        else:
                            packed = jnp.where(z_third == exit_z - sign * (q + g), piece, packed)
            out_z[step, at, side] = packed
            send(step, group, (0, 0, sign), out_z.at[step, at, side], got_z.at[step, at, side])
        for side, sign in enumerate((1, -1)):
            col = LANES - 128 if sign == 1 else 0
            for k, i in enumerate(with_component(1, sign)):
                for t in tiles:
                    out_y[step, at, side, k, SPOT[t] : SPOT[t] + 8, :] = post[
                        step, i, padded(t), col : col + 128
                    ]
            send(
                step,
                group,
                (0, sign, 0),
                out_y.at[step, at, side, :, begin:end, :],
                got_y.at[step, at, side, :, begin:end, :],
            )
        for i in range(15, 19):
            col = LANES - 128 if VELS[i][1] == 1 else 0
            for t in tiles:
                out_yz[step, at, i - 15, SPOT[t] : SPOT[t] + 8, :] = post[
                    step, i, padded(t), col : col + 128
                ]
            send(
                step,
                group,
                VELS[i],
                out_yz.at[step, at, i - 15, begin:end, :],
                got_yz.at[step, at, i - 15, begin:end, :],
            )

    def fill_yz(step, group, tiles):
        at = 1 if group == "inner" else 0
        tile_lane = lane[:, :128]
        for n, t in enumerate(tiles):
            spot = slice(SPOT[t], SPOT[t] + 8)
            for i in range(3, 19):
                cx, cy, cz = VELS[i]
                if cz:
                    exit_z = ROW - 1 if cz == 1 else 0
                    side = 0 if cz == 1 else 1
                    q = 3 * (5 * n + with_component(2, cz).index(i))
                    packed = got_z[step, at, side]
                    parts = [
                        pltpu.roll(packed, (cz * (q + g)) % THIRD, 1) if q + g else packed
                        for g in range(3)
                    ]
                    post[step, i, padded(t), :] = jnp.where(
                        z == exit_z, jnp.concatenate(parts, axis=1), post[step, i, padded(t), :]
                    )
                if cy:
                    side = 0 if cy == 1 else 1
                    col = LANES - 128 if cy == 1 else 0
                    cols = slice(col, col + 128)
                    leaves = tile_lane >= 128 - ROW if cy == 1 else tile_lane < ROW
                    if cz:
                        leaves = leaves & (z[:, cols] != exit_z)
                    k = with_component(1, cy).index(i)
                    post[step, i, padded(t), cols] = jnp.where(
                        leaves, got_y[step, at, side, k, spot, :], post[step, i, padded(t), cols]
                    )
                if cy and cz:
                    from_y = BS - 1 if cy == 1 else 0
                    slot = ((from_y - cz) % BS) * ROW + exit_z
                    source = from_y * ROW + exit_z
                    cols = slice(slot // 128 * 128, slot // 128 * 128 + 128)
                    edge = pltpu.roll(got_yz[step, at, i - 15, spot, :], (slot - source) % 128, 1)
                    post[step, i, padded(t), cols] = jnp.where(
                        tile_lane == slot % 128, edge, post[step, i, padded(t), cols]
                    )

    def fill_x(step, sign):
        side = 0 if sign == 1 else 1
        row_at = PAD - 1 if sign == 1 else PAD + BS
        one_lane = lane[0:1]
        for k, i in enumerate(with_component(0, sign)):
            cx, cy, cz = VELS[i]
            row = got_x[step, side, k : k + 1, :]
            if cz:
                exit_z = ROW - 1 if cz == 1 else 0
                edge = pltpu.roll(got_xz[step, i - 11], (-cz * ROW) % LANES, 1)
                row = jnp.where(z[0:1] == exit_z, edge, row)
            post[step, i, row_at : row_at + 1, :] = row
            if cy:
                col = LANES - 128 if cy == 1 else 0
                cols = slice(col, col + 128)
                leaves = one_lane[:, :128] >= 128 - ROW if cy == 1 else one_lane[:, :128] < ROW
                post[step, i, row_at : row_at + 1, cols] = jnp.where(
                    leaves, got_xy[step, i - 7], row[:, cols]
                )

    def stream(step, t, which=range(19)):
        target = fields if step == STEPS - 1 else flow
        for i in which:
            cx, cy, cz = VELS[i]
            v = post[step, i, padded(t, -cx), :]
            shift = (cy * ROW + cz) % LANES
            target[i, rows_of(t), :] = pltpu.roll(v, shift, 1) if shift else v

    loads[1].wait()
    pack(0, (18, 0), (18, 1))
    pack(1, (18, 2), None)
    loads[2].wait()
    pack_tile(0)
    pl.semaphore_wait(barrier, len(partners))
    send_ring(0, slice(0, FIRST_ROW[0] + 9), slice(0, 8))
    loads[3].wait()
    pack_tile(2)
    send_ring(1, slice(FIRST_ROW[2], FIRST_ROW[2] + 9), slice(0, 8))
    loads[4].wait()
    pack_tile(1)
    middle = slice(FIRST_ROW[1], FIRST_ROW[1] + 9)
    send_ring(2, middle, slice(0, 1))
    send_ring(3, middle, slice(7, 8))
    send_ring(4, middle, slice(1, 7))
    loads[5].wait()

    await_ring(0)
    unpack(0, (18, 0), (18, 1))
    unpack(1, (18, 2), None)
    unpack_tile(0)
    collide_tile(0, 0)
    send_x(0, -1)
    await_ring(1)
    unpack_tile(2)
    collide_tile(0, 2)
    send_x(0, 1)
    await_ring(2)
    await_ring(3)
    unpack_tile(1, slice(0, 1))
    unpack_tile(1, slice(7, 8))
    collide_tile(0, 1)
    send_yz(0, "outer", (0, 2, 1))
    await_halo(0, "outer")
    fill_yz(0, "outer", (0, 2, 1))
    await_halo(0, ("x", -1))
    fill_x(0, -1)
    stream(0, 2)
    collide_tile(1, 2)
    send_x(1, 1)
    stream(0, 0)

    await_ring(4)
    unpack_tile(1)
    collide_tile(0, 1)
    send_yz(0, "inner", (1,))

    await_halo(0, ("x", 1))
    fill_x(0, 1)
    for i in with_component(0, 1):
        cx, cy, cz = VELS[i]
        shift = (cy * ROW + cz) % LANES
        row = post[0, i, PAD - 1 : PAD, :]
        flow[i, 0:1, :] = pltpu.roll(row, shift, 1) if shift else row
    collide_tile(1, 0)
    send_x(1, -1)
    send_yz(1, "outer", (0, 2))

    await_halo(0, "inner")
    fill_yz(0, "inner", (1,))
    stream(0, 1)
    collide_tile(1, 1)
    send_yz(1, "inner", (1,))

    await_halo(1, "outer")
    fill_yz(1, "outer", (0, 2))
    await_halo(1, ("x", 1))
    fill_x(1, 1)
    stream(1, 0, [i for i in range(19) if VELS[i][0] != -1])
    await_halo(1, ("x", -1))
    fill_x(1, -1)
    stream(1, 2, [i for i in range(19) if VELS[i][0] != 1])
    await_halo(1, "inner")
    fill_yz(1, "inner", (1,))
    stream(1, 1)
    stream(1, 0, with_component(0, -1))
    stream(1, 2, with_component(0, 1))
    for copies in list(ring.values()) + list(started.values()):
        for copy in copies:
            copy.wait_send()


def per_device(popul, codes, solid):
    vmem = pl.BlockSpec(memory_space=pltpu.VMEM)
    fields = pl.pallas_call(
        kernel,
        out_shape=jax.ShapeDtypeStruct((19, BS, LANES), jnp.float32),
        in_specs=[pl.BlockSpec(memory_space=pltpu.HBM)] * 3,
        out_specs=vmem,
        scratch_shapes=[
            pltpu.SMEM((2,), jnp.int32),
            pltpu.VMEM((BS, LANES), jnp.int32),
            pltpu.VMEM((19, BS, LANES), jnp.float32),
            pltpu.VMEM((19, BS, LANES), jnp.float32),
            pltpu.VMEM((19, BS, LANES), jnp.float32),
            pltpu.VMEM((STEPS, 19, BS + 2 * PAD, LANES), jnp.float32),
        ]
        + [pltpu.VMEM((PACKED, 8, LANES), jnp.float32)] * 4
        + [
            pltpu.VMEM((STEPS, 2, 5, LANES), jnp.float32),
            pltpu.VMEM((STEPS, 2, 2, 5, BS, 128), jnp.float32),
            pltpu.VMEM((STEPS, 2, 2, 8, THIRD), jnp.float32),
            pltpu.VMEM((STEPS, 2, 4, BS, 128), jnp.float32),
        ]
        * 2
        + [
            pltpu.VMEM((STEPS, 4, 1, 128), jnp.float32),
            pltpu.VMEM((STEPS, 4, 1, LANES), jnp.float32),
            pltpu.SemaphoreType.DMA((6,)),
            pltpu.SemaphoreType.DMA((2, 5)),
            pltpu.SemaphoreType.DMA((2, 5)),
            pltpu.SemaphoreType.DMA((STEPS, 36)),
            pltpu.SemaphoreType.DMA((STEPS, 36)),
        ],
        compiler_params=pltpu.CompilerParams(
            collective_id=0, has_side_effects=True, vmem_limit_bytes=51 * 1024 * 1024
        ),
        cost_estimate=pl.CostEstimate(flops=14_000_000, bytes_accessed=4_500_000, transcendentals=0),
    )(codes, popul.reshape(19, BS, LANES), solid.reshape(BS, LANES))
    return fields.reshape(popul.shape)


def solution(mesh):
    placed = (
        P("gx", "gy", "gz", None, None),
        P(("gx", "gy", "gz")),
        P("gx", "gy", "gz", None, None),
    )
    return jax.shard_map(
        per_device,
        mesh=mesh,
        in_specs=placed,
        out_specs=P("gx", "gy", "gz", None, None),
        check_vma=False,
    )
```

```python
import functools

import jax
import jax.numpy as jnp
from jax import lax
from jax.experimental import pallas as pl
from jax.experimental.pallas import tpu as pltpu
from jax.sharding import PartitionSpec as P

STEPS = 2
VELS = [
    (0, 0, 0),
    (1, 0, 0),
    (-1, 0, 0),
    (0, 1, 0),
    (0, -1, 0),
    (0, 0, 1),
    (0, 0, -1),
    (1, 1, 0),
    (-1, -1, 0),
    (1, -1, 0),
    (-1, 1, 0),
    (1, 0, 1),
    (-1, 0, -1),
    (1, 0, -1),
    (-1, 0, 1),
    (0, 1, 1),
    (0, -1, -1),
    (0, 1, -1),
    (0, -1, 1),
]
WEIGHTS = [1.0 / 3.0] + [1.0 / 18.0] * 6 + [1.0 / 36.0] * 12
OPPOSITE = [VELS.index((-a, -b, -c)) for a, b, c in VELS]
OMEGA = 1.25
MESH = pl.DeviceIdType.MESH
DIRS = VELS[1:]
BS = 24
ROW = 2 * BS
LANES = BS * ROW
TILES = BS // 8
COLS = LANES // 128
THIRD = LANES // 3
PAD = 8
SPOT = {0: 0, 2: 8, 1: 16}
FIRST_ROW = {0: 1, 2: 10, 1: 19}
FOLDED = 28
HALF = LANES // 2
HALF_COLS = 640
PACKED = 29


def with_component(axis, sign):
    return [i for i, c in enumerate(VELS) if c[axis] == sign]


def place_of(delta):
    sx, sy, sz = (lax.axis_size(a) for a in ("gx", "gy", "gz"))
    x, y, z = (lax.axis_index(a) for a in ("gx", "gy", "gz"))
    total = sx * sy * sz
    p = lax.rem((x * sy + y) * sz + z + (delta + total), total)
    return (p // (sy * sz), lax.rem(p // sz, sy), lax.rem(p, sz))


def beside(c):
    place = []
    for axis, by in zip(("gx", "gy", "gz"), c):
        size = lax.axis_size(axis)
        place.append(lax.rem(lax.axis_index(axis) + (by + size), size))
    return tuple(place)


def collide(f, solid):
    rho = functools.reduce(lambda a, b: a + b, f)
    inv = 1.0 / rho
    vel = []
    for axis in range(3):
        plus = [f[i] for i in with_component(axis, 1)]
        minus = [f[i] for i in with_component(axis, -1)]
        vel.append((sum(plus[1:], plus[0]) - sum(minus[1:], minus[0])) * inv)
    speed = vel[0] * vel[0] + vel[1] * vel[1] + vel[2] * vel[2]
    base = 1.0 - 1.5 * speed
    bounce = solid == 1
    posts = [None] * 19
    weighted = {w: (OMEGA * w) * rho for w in set(WEIGHTS)}
    for i in range(19):
        if posts[i] is not None:
            continue
        o = OPPOSITE[i]
        w = weighted[WEIGHTS[i]]
        if i == o:
            posts[i] = jnp.where(bounce, f[i], (1.0 - OMEGA) * f[i] + w * base)
            continue
        along = None
        for axis in range(3):
            if VELS[i][axis] == 1:
                along = vel[axis] if along is None else along + vel[axis]
            elif VELS[i][axis] == -1:
                along = -vel[axis] if along is None else along - vel[axis]
        even = w * (base + 4.5 * (along * along))
        odd = (3.0 * w) * along
        posts[i] = jnp.where(bounce, f[o], (1.0 - OMEGA) * f[i] + (even + odd))
        posts[o] = jnp.where(bounce, f[i], (1.0 - OMEGA) * f[o] + (even - odd))
    return posts


def kernel(
    held_codes, popul, held_solid, fields,
    codes, solid, cells, home, flow, post, send_up, send_down, got_up, got_down,
    out_x, out_y, out_z, out_yz, got_x, got_y, got_z, got_yz, got_xy, got_xz,
    load_sem, ring_send, ring_recv, halo_send, halo_recv,
):
    def rows_of(t):
        return slice(8 * t, 8 * t + 8)

    def padded(t, by=0):
        return slice(PAD + 8 * t + by, PAD + 8 * t + 8 + by)

    sources = [
        (held_codes, codes),
        (popul.at[18], cells.at[18]),
        (popul.at[0:18, rows_of(0)], cells.at[0:18, rows_of(0)]),
        (popul.at[0:18, rows_of(2)], cells.at[0:18, rows_of(2)]),
        (popul.at[0:18, rows_of(1)], cells.at[0:18, rows_of(1)]),
        (held_solid, solid),
    ]
    loads = [
        pltpu.make_async_copy(source, target, load_sem.at[n])
        for n, (source, target) in enumerate(sources)
    ]
    for load in loads:
        load.start()
    following, previous = place_of(1), place_of(-1)
    partners = [following, previous] + [beside(c) for c in DIRS]
    barrier = pltpu.get_barrier_semaphore()
    for partner in partners:
        pl.semaphore_signal(barrier, inc=1, device_id=partner, device_id_type=MESH)

    lane = lax.broadcasted_iota(jnp.int32, (8, LANES), 1)
    z = lax.rem(lane, ROW)
    z_third = z[:, :THIRD]
    first = z < BS
    loads[0].wait()
    low_code = jnp.minimum(codes[0], codes[1])
    high_code = jnp.maximum(codes[0], codes[1])
    ordered = jnp.broadcast_to(codes[1], (8, LANES)) >= 3
    from_low = first & (jnp.broadcast_to(low_code, (8, LANES)) == 1)
    from_high = jnp.logical_not(first) & (jnp.broadcast_to(high_code, (8, LANES)) == 4)

    def both_orders(i, t):
        a = cells[i, rows_of(t), :]
        w = jnp.where(first, pltpu.roll(a, LANES - BS, 1), pltpu.roll(a, BS, 1))
        normal = jnp.where(ordered, a, w)
        home[i, rows_of(t), :] = normal
        return normal, jnp.where(ordered, w, a)

    def pack(row, one, two):
        normal_one, swapped_one = both_orders(*one)
        normal_two, swapped_two = both_orders(*two)
        send_up[row] = jnp.where(first, swapped_one, normal_two)
        send_down[row] = jnp.where(first, normal_one, swapped_two)

    def pack_folded(i, t):
        normal, swapped = both_orders(i, t)
        folded = pltpu.roll(normal, LANES - HALF, 1)
        send_up[FOLDED] = jnp.where(first, swapped, folded)
        send_down[FOLDED] = jnp.where(first, folded, swapped)

    def unpack_folded(i, t):
        low, high = got_up[FOLDED], got_down[FOLDED]
        low = jnp.where(lane < HALF, low, pltpu.roll(low, HALF - BS, 1))
        high = jnp.where(lane < HALF, high, pltpu.roll(high, HALF + BS, 1))
        own = jnp.where(from_low, low, home[i, rows_of(t), :])
        home[i, rows_of(t), :] = jnp.where(from_high, high, own)

    def pack_tile(t):
        for k in range(9):
            pack(FIRST_ROW[t] + k, (2 * k, t), (2 * k + 1, t))

    ring = {}

    def send_ring(n, rows, planes, cols=slice(0, LANES)):
        pair = []
        for way, (source, target, device) in enumerate(
            ((send_up, got_up, following), (send_down, got_down, previous))
        ):
            copy = pltpu.make_async_remote_copy(
                src_ref=source.at[rows, planes, cols],
                dst_ref=target.at[rows, planes, cols],
                send_sem=ring_send.at[way, n],
                recv_sem=ring_recv.at[way, n],
                device_id=device,
                device_id_type=MESH,
            )
            copy.start()
            pair.append(copy)
        ring[n] = pair

    def await_ring(n):
        for copy in ring[n]:
            copy.wait_recv()

    def unpack(row, one, two, planes=slice(0, 8)):
        low, high = got_up[row, planes, :], got_down[row, planes, :]
        i, t = one
        here = slice(8 * t + planes.start, 8 * t + planes.stop)
        own = jnp.where(from_low[planes], low, home[i, here, :])
        home[i, here, :] = jnp.where(from_high[planes], pltpu.roll(high, BS, 1), own)
        i, t = two
        here = slice(8 * t + planes.start, 8 * t + planes.stop)
        own = jnp.where(from_low[planes], pltpu.roll(low, LANES - BS, 1), home[i, here, :])
        home[i, here, :] = jnp.where(from_high[planes], high, own)

    def unpack_tile(t, planes=slice(0, 8)):
        for k in range(9):
            unpack(FIRST_ROW[t] + k, (2 * k, t), (2 * k + 1, t), planes)

    def collide_tile(step, t):
        source = home if step == 0 else flow

        def one_column(j, carry):
            cols = pl.ds(pl.multiple_of(j * 128, 128), 128)
            posts = collide([source[i, rows_of(t), cols] for i in range(19)], solid[rows_of(t), cols])
            for i in range(19):
                post[step, i, padded(t), cols] = posts[i]
            return carry

        lax.fori_loop(0, COLS, one_column, 0, unroll=True)

    started = {}

    def send(step, group, c, source, target):
        n = DIRS.index(c) + (18 if group == "inner" else 0)
        copy = pltpu.make_async_remote_copy(
            src_ref=source,
            dst_ref=target,
            send_sem=halo_send.at[step, n],
            recv_sem=halo_recv.at[step, n],
            device_id=beside(c),
            device_id_type=MESH,
        )
        copy.start()
        started.setdefault((step, group), []).append(copy)

    def await_halo(step, group):
        for copy in started[step, group]:
            copy.wait_recv()

    def send_x(step, sign):
        side = 0 if sign == 1 else 1
        exit_x = PAD + (BS - 1 if sign == 1 else 0)
        group = ("x", sign)
        for k, i in enumerate(with_component(0, sign)):
            out_x[step, side, k : k + 1, :] = post[step, i, exit_x : exit_x + 1, :]
        send(step, group, (sign, 0, 0), out_x.at[step, side], got_x.at[step, side])
        for k, i in enumerate(with_component(0, sign)):
            cx, cy, cz = VELS[i]
            if cy:
                cols = slice(LANES - 128, LANES) if cy == 1 else slice(0, 128)
                send(step, group, VELS[i], out_x.at[step, side, k : k + 1, cols], got_xy.at[step, i - 7])
            if cz:
                send(step, group, VELS[i], out_x.at[step, side, k : k + 1, :], got_xz.at[step, i - 11])

    def send_yz(step, group, tiles):
        at = 1 if group == "inner" else 0
        begin, end = SPOT[tiles[0]], SPOT[tiles[-1]] + 8
        for side, sign in enumerate((1, -1)):
            exit_z = ROW - 1 if sign == 1 else 0
            packed = None
            for n, t in enumerate(tiles):
                for k, i in enumerate(with_component(2, sign)):
                    q = 3 * (5 * n + k)
                    part = post[step, i, padded(t), :]
                    for g in range(3):
                        turned = pltpu.roll(part, (-sign * (ROW + q + g)) % LANES, 1)
                        piece = turned[:, THIRD * g : THIRD * g + THIRD]
                        if packed is None:
                            packed = piece
                        else:
                            packed = jnp.where(z_third == exit_z - sign * (q + g), piece, packed)
            out_z[step, at, side] = packed
            send(step, group, (0, 0, sign), out_z.at[step, at, side], got_z.at[step, at, side])
        for side, sign in enumerate((1, -1)):
            col = LANES - 128 if sign == 1 else 0
            for k, i in enumerate(with_component(1, sign)):
                for t in tiles:
                    out_y[step, at, side, k, SPOT[t] : SPOT[t] + 8, :] = post[
                        step, i, padded(t), col : col + 128
                    ]
            send(
                step,
                group,
                (0, sign, 0),
                out_y.at[step, at, side, :, begin:end, :],
                got_y.at[step, at, side, :, begin:end, :],
            )
        for i in range(15, 19):
            col = LANES - 128 if VELS[i][1] == 1 else 0
            for t in tiles:
                out_yz[step, at, i - 15, SPOT[t] : SPOT[t] + 8, :] = post[
                    step, i, padded(t), col : col + 128
                ]
            send(
                step,
                group,
                VELS[i],
                out_yz.at[step, at, i - 15, begin:end, :],
                got_yz.at[step, at, i - 15, begin:end, :],
            )

    def fill_yz(step, group, tiles):
        at = 1 if group == "inner" else 0
        tile_lane = lane[:, :128]
        for n, t in enumerate(tiles):
            spot = slice(SPOT[t], SPOT[t] + 8)
            for i in range(3, 19):
                cx, cy, cz = VELS[i]
                if cz:
                    exit_z = ROW - 1 if cz == 1 else 0
                    side = 0 if cz == 1 else 1
                    q = 3 * (5 * n + with_component(2, cz).index(i))
                    packed = got_z[step, at, side]
                    parts = [
                        pltpu.roll(packed, (cz * (q + g)) % THIRD, 1) if q + g else packed
                        for g in range(3)
                    ]
                    post[step, i, padded(t), :] = jnp.where(
                        z == exit_z, jnp.concatenate(parts, axis=1), post[step, i, padded(t), :]
                    )
                if cy:
                    side = 0 if cy == 1 else 1
                    col = LANES - 128 if cy == 1 else 0
                    cols = slice(col, col + 128)
                    leaves = tile_lane >= 128 - ROW if cy == 1 else tile_lane < ROW
                    if cz:
                        leaves = leaves & (z[:, cols] != exit_z)
                    k = with_component(1, cy).index(i)
                    post[step, i, padded(t), cols] = jnp.where(
                        leaves, got_y[step, at, side, k, spot, :], post[step, i, padded(t), cols]
                    )
                if cy and cz:
                    from_y = BS - 1 if cy == 1 else 0
                    slot = ((from_y - cz) % BS) * ROW + exit_z
                    source = from_y * ROW + exit_z
                    cols = slice(slot // 128 * 128, slot // 128 * 128 + 128)
                    edge = pltpu.roll(got_yz[step, at, i - 15, spot, :], (slot - source) % 128, 1)
                    post[step, i, padded(t), cols] = jnp.where(
                        tile_lane == slot % 128, edge, post[step, i, padded(t), cols]
                    )

    def fill_x(step, sign):
        side = 0 if sign == 1 else 1
        row_at = PAD - 1 if sign == 1 else PAD + BS
        one_lane = lane[0:1]
        for k, i in enumerate(with_component(0, sign)):
            cx, cy, cz = VELS[i]
            row = got_x[step, side, k : k + 1, :]
            if cz:
                exit_z = ROW - 1 if cz == 1 else 0
                edge = pltpu.roll(got_xz[step, i - 11], (-cz * ROW) % LANES, 1)
                row = jnp.where(z[0:1] == exit_z, edge, row)
            post[step, i, row_at : row_at + 1, :] = row
            if cy:
                col = LANES - 128 if cy == 1 else 0
                cols = slice(col, col + 128)
                leaves = one_lane[:, :128] >= 128 - ROW if cy == 1 else one_lane[:, :128] < ROW
                post[step, i, row_at : row_at + 1, cols] = jnp.where(
                    leaves, got_xy[step, i - 7], row[:, cols]
                )

    def stream(step, t, which=range(19)):
        target = fields if step == STEPS - 1 else flow
        for i in which:
            cx, cy, cz = VELS[i]
            v = post[step, i, padded(t, -cx), :]
            shift = (cy * ROW + cz) % LANES
            target[i, rows_of(t), :] = pltpu.roll(v, shift, 1) if shift else v

    loads[1].wait()
    pack(0, (18, 0), (18, 1))
    pack_folded(18, 2)
    loads[2].wait()
    pack_tile(0)
    pl.semaphore_wait(barrier, len(partners))
    send_ring(0, slice(0, FIRST_ROW[0] + 9), slice(0, 8))
    send_ring(5, slice(FOLDED, FOLDED + 1), slice(0, 8), slice(0, HALF_COLS))
    loads[3].wait()
    pack_tile(2)
    send_ring(1, slice(FIRST_ROW[2], FIRST_ROW[2] + 9), slice(0, 8))
    loads[4].wait()
    pack_tile(1)
    middle = slice(FIRST_ROW[1], FIRST_ROW[1] + 9)
    send_ring(2, middle, slice(0, 1))
    send_ring(3, middle, slice(7, 8))
    send_ring(4, middle, slice(1, 7))
    loads[5].wait()

    await_ring(0)
    await_ring(5)
    unpack(0, (18, 0), (18, 1))
    unpack_folded(18, 2)
    unpack_tile(0)
    collide_tile(0, 0)
    send_x(0, -1)
    await_ring(1)
    unpack_tile(2)
    collide_tile(0, 2)
    send_x(0, 1)
    await_ring(2)
    await_ring(3)
    unpack_tile(1, slice(0, 1))
    unpack_tile(1, slice(7, 8))
    collide_tile(0, 1)
    send_yz(0, "outer", (0, 2, 1))

    await_ring(4)
    unpack_tile(1)
    collide_tile(0, 1)
    send_yz(0, "inner", (1,))

    await_halo(0, "outer")
    fill_yz(0, "outer", (0, 2, 1))
    await_halo(0, ("x", -1))
    fill_x(0, -1)
    stream(0, 2)
    collide_tile(1, 2)
    send_x(1, 1)
    await_halo(0, ("x", 1))
    fill_x(0, 1)
    stream(0, 0)
    collide_tile(1, 0)
    send_x(1, -1)
    send_yz(1, "outer", (0, 2))

    await_halo(0, "inner")
    fill_yz(0, "inner", (1,))
    stream(0, 1)
    collide_tile(1, 1)
    send_yz(1, "inner", (1,))

    await_halo(1, "outer")
    fill_yz(1, "outer", (0, 2))
    await_halo(1, ("x", 1))
    fill_x(1, 1)
    stream(1, 0, [i for i in range(19) if VELS[i][0] != -1])
    await_halo(1, ("x", -1))
    fill_x(1, -1)
    stream(1, 2, [i for i in range(19) if VELS[i][0] != 1])
    await_halo(1, "inner")
    fill_yz(1, "inner", (1,))
    stream(1, 1)
    stream(1, 0, with_component(0, -1))
    stream(1, 2, with_component(0, 1))
    for copies in list(ring.values()) + list(started.values()):
        for copy in copies:
            copy.wait_send()


def per_device(popul, codes, solid):
    vmem = pl.BlockSpec(memory_space=pltpu.VMEM)
    fields = pl.pallas_call(
        kernel,
        out_shape=jax.ShapeDtypeStruct((19, BS, LANES), jnp.float32),
        in_specs=[pl.BlockSpec(memory_space=pltpu.HBM)] * 3,
        out_specs=vmem,
        scratch_shapes=[
            pltpu.SMEM((2,), jnp.int32),
            pltpu.VMEM((BS, LANES), jnp.int32),
            pltpu.VMEM((19, BS, LANES), jnp.float32),
            pltpu.VMEM((19, BS, LANES), jnp.float32),
            pltpu.VMEM((19, BS, LANES), jnp.float32),
            pltpu.VMEM((STEPS, 19, BS + 2 * PAD, LANES), jnp.float32),
        ]
        + [pltpu.VMEM((PACKED, 8, LANES), jnp.float32)] * 4
        + [
            pltpu.VMEM((STEPS, 2, 5, LANES), jnp.float32),
            pltpu.VMEM((STEPS, 2, 2, 5, BS, 128), jnp.float32),
            pltpu.VMEM((STEPS, 2, 2, 8, THIRD), jnp.float32),
            pltpu.VMEM((STEPS, 2, 4, BS, 128), jnp.float32),
        ]
        * 2
        + [
            pltpu.VMEM((STEPS, 4, 1, 128), jnp.float32),
            pltpu.VMEM((STEPS, 4, 1, LANES), jnp.float32),
            pltpu.SemaphoreType.DMA((6,)),
            pltpu.SemaphoreType.DMA((2, 6)),
            pltpu.SemaphoreType.DMA((2, 6)),
            pltpu.SemaphoreType.DMA((STEPS, 36)),
            pltpu.SemaphoreType.DMA((STEPS, 36)),
        ],
        compiler_params=pltpu.CompilerParams(
            collective_id=0, has_side_effects=True, vmem_limit_bytes=51 * 1024 * 1024
        ),
        cost_estimate=pl.CostEstimate(flops=14_000_000, bytes_accessed=4_500_000, transcendentals=0),
    )(codes, popul.reshape(19, BS, LANES), solid.reshape(BS, LANES))
    return fields.reshape(popul.shape)


def solution(mesh):
    placed = (
        P("gx", "gy", "gz", None, None),
        P(("gx", "gy", "gz")),
        P("gx", "gy", "gz", None, None),
    )
    return jax.shard_map(
        per_device,
        mesh=mesh,
        in_specs=placed,
        out_specs=P("gx", "gy", "gz", None, None),
        check_vma=False,
    )
```

```python
import functools

import jax
import jax.numpy as jnp
from jax import lax
from jax.experimental import pallas as pl
from jax.experimental.pallas import tpu as pltpu
from jax.sharding import PartitionSpec as P

STEPS = 2
VELS = [
    (0, 0, 0),
    (1, 0, 0),
    (-1, 0, 0),
    (0, 1, 0),
    (0, -1, 0),
    (0, 0, 1),
    (0, 0, -1),
    (1, 1, 0),
    (-1, -1, 0),
    (1, -1, 0),
    (-1, 1, 0),
    (1, 0, 1),
    (-1, 0, -1),
    (1, 0, -1),
    (-1, 0, 1),
    (0, 1, 1),
    (0, -1, -1),
    (0, 1, -1),
    (0, -1, 1),
]
WEIGHTS = [1.0 / 3.0] + [1.0 / 18.0] * 6 + [1.0 / 36.0] * 12
OPPOSITE = [VELS.index((-a, -b, -c)) for a, b, c in VELS]
OMEGA = 1.25
MESH = pl.DeviceIdType.MESH
DIRS = VELS[1:]
BS = 24
ROW = 2 * BS
LANES = BS * ROW
TILES = BS // 8
COLS = LANES // 128
THIRD = LANES // 3
PAD = 8
SPOT = {0: 0, 2: 8, 1: 16}
FIRST_ROW = {0: 1, 2: 10, 1: 19}
FOLDED = 28
HALF = LANES // 2
HALF_COLS = 640
PACKED = 29


def with_component(axis, sign):
    return [i for i, c in enumerate(VELS) if c[axis] == sign]


def place_of(delta):
    sx, sy, sz = (lax.axis_size(a) for a in ("gx", "gy", "gz"))
    x, y, z = (lax.axis_index(a) for a in ("gx", "gy", "gz"))
    total = sx * sy * sz
    p = lax.rem((x * sy + y) * sz + z + (delta + total), total)
    return (p // (sy * sz), lax.rem(p // sz, sy), lax.rem(p, sz))


def beside(c):
    place = []
    for axis, by in zip(("gx", "gy", "gz"), c):
        size = lax.axis_size(axis)
        place.append(lax.rem(lax.axis_index(axis) + (by + size), size))
    return tuple(place)


def collide(f, solid):
    rho = functools.reduce(lambda a, b: a + b, f)
    inv = 1.0 / rho
    vel = []
    for axis in range(3):
        plus = [f[i] for i in with_component(axis, 1)]
        minus = [f[i] for i in with_component(axis, -1)]
        vel.append((sum(plus[1:], plus[0]) - sum(minus[1:], minus[0])) * inv)
    speed = vel[0] * vel[0] + vel[1] * vel[1] + vel[2] * vel[2]
    base = 1.0 - 1.5 * speed
    bounce = solid == 1
    posts = [None] * 19
    weighted = {w: (OMEGA * w) * rho for w in set(WEIGHTS)}
    for i in range(19):
        if posts[i] is not None:
            continue
        o = OPPOSITE[i]
        w = weighted[WEIGHTS[i]]
        if i == o:
            posts[i] = jnp.where(bounce, f[i], (1.0 - OMEGA) * f[i] + w * base)
            continue
        along = None
        for axis in range(3):
            if VELS[i][axis] == 1:
                along = vel[axis] if along is None else along + vel[axis]
            elif VELS[i][axis] == -1:
                along = -vel[axis] if along is None else along - vel[axis]
        even = w * (base + 4.5 * (along * along))
        odd = (3.0 * w) * along
        posts[i] = jnp.where(bounce, f[o], (1.0 - OMEGA) * f[i] + (even + odd))
        posts[o] = jnp.where(bounce, f[i], (1.0 - OMEGA) * f[o] + (even - odd))
    return posts


def kernel(
    held_codes, popul, held_solid, fields,
    codes, solid, cells, home, flow, post, send_up, send_down, got_up, got_down,
    out_x, out_y, out_z, out_yz, got_x, got_y, got_z, got_yz, got_xy, got_xz,
    load_sem, ring_send, ring_recv, halo_send, halo_recv,
):
    def rows_of(t):
        return slice(8 * t, 8 * t + 8)

    def padded(t, by=0):
        return slice(PAD + 8 * t + by, PAD + 8 * t + 8 + by)

    sources = [
        (held_codes, codes),
        (popul.at[18], cells.at[18]),
        (popul.at[0:18, rows_of(0)], cells.at[0:18, rows_of(0)]),
        (popul.at[0:18, rows_of(2)], cells.at[0:18, rows_of(2)]),
        (popul.at[0:18, rows_of(1)], cells.at[0:18, rows_of(1)]),
        (held_solid, solid),
    ]
    loads = [
        pltpu.make_async_copy(source, target, load_sem.at[n])
        for n, (source, target) in enumerate(sources)
    ]
    for load in loads:
        load.start()
    following, previous = place_of(1), place_of(-1)
    partners = [following, previous] + [beside(c) for c in DIRS]
    barrier = pltpu.get_barrier_semaphore()
    for partner in partners:
        pl.semaphore_signal(barrier, inc=1, device_id=partner, device_id_type=MESH)

    lane = lax.broadcasted_iota(jnp.int32, (8, LANES), 1)
    z = lax.rem(lane, ROW)
    z_third = z[:, :THIRD]
    first = z < BS
    loads[0].wait()
    low_code = jnp.minimum(codes[0], codes[1])
    high_code = jnp.maximum(codes[0], codes[1])
    ordered = jnp.broadcast_to(codes[1], (8, LANES)) >= 3
    from_low = first & (jnp.broadcast_to(low_code, (8, LANES)) == 1)
    from_high = jnp.logical_not(first) & (jnp.broadcast_to(high_code, (8, LANES)) == 4)

    def both_orders(i, t):
        a = cells[i, rows_of(t), :]
        w = jnp.where(first, pltpu.roll(a, LANES - BS, 1), pltpu.roll(a, BS, 1))
        normal = jnp.where(ordered, a, w)
        home[i, rows_of(t), :] = normal
        return normal, jnp.where(ordered, w, a)

    def pack(row, one, two):
        normal_one, swapped_one = both_orders(*one)
        normal_two, swapped_two = both_orders(*two)
        send_up[row] = jnp.where(first, swapped_one, normal_two)
        send_down[row] = jnp.where(first, normal_one, swapped_two)

    def pack_folded(i, t):
        normal, swapped = both_orders(i, t)
        folded = pltpu.roll(normal, LANES - HALF, 1)
        send_up[FOLDED] = jnp.where(first, swapped, folded)
        send_down[FOLDED] = jnp.where(first, folded, swapped)

    def unpack_folded(i, t):
        low, high = got_up[FOLDED], got_down[FOLDED]
        low = jnp.where(lane < HALF, low, pltpu.roll(low, HALF - BS, 1))
        high = jnp.where(lane < HALF, high, pltpu.roll(high, HALF + BS, 1))
        own = jnp.where(from_low, low, home[i, rows_of(t), :])
        home[i, rows_of(t), :] = jnp.where(from_high, high, own)

    def pack_tile(t):
        for k in range(9):
            pack(FIRST_ROW[t] + k, (2 * k, t), (2 * k + 1, t))

    ring = {}

    def send_ring(n, rows, planes, cols=slice(0, LANES)):
        pair = []
        for way, (source, target, device) in enumerate(
            ((send_up, got_up, following), (send_down, got_down, previous))
        ):
            copy = pltpu.make_async_remote_copy(
                src_ref=source.at[rows, planes, cols],
                dst_ref=target.at[rows, planes, cols],
                send_sem=ring_send.at[way, n],
                recv_sem=ring_recv.at[way, n],
                device_id=device,
                device_id_type=MESH,
            )
            copy.start()
            pair.append(copy)
        ring[n] = pair

    def await_ring(n):
        for copy in ring[n]:
            copy.wait_recv()

    def unpack(row, one, two, planes=slice(0, 8)):
        low, high = got_up[row, planes, :], got_down[row, planes, :]
        i, t = one
        here = slice(8 * t + planes.start, 8 * t + planes.stop)
        own = jnp.where(from_low[planes], low, home[i, here, :])
        home[i, here, :] = jnp.where(from_high[planes], pltpu.roll(high, BS, 1), own)
        i, t = two
        here = slice(8 * t + planes.start, 8 * t + planes.stop)
        own = jnp.where(from_low[planes], pltpu.roll(low, LANES - BS, 1), home[i, here, :])
        home[i, here, :] = jnp.where(from_high[planes], high, own)

    def unpack_tile(t, planes=slice(0, 8)):
        for k in range(9):
            unpack(FIRST_ROW[t] + k, (2 * k, t), (2 * k + 1, t), planes)

    def collide_tile(step, t):
        source = home if step == 0 else flow

        def one_column(j, carry):
            cols = pl.ds(pl.multiple_of(j * 128, 128), 128)
            posts = collide([source[i, rows_of(t), cols] for i in range(19)], solid[rows_of(t), cols])
            for i in range(19):
                post[step, i, padded(t), cols] = posts[i]
            return carry

        lax.fori_loop(0, COLS, one_column, 0, unroll=True)

    started = {}

    def send(step, group, c, source, target):
        n = DIRS.index(c) + (18 if group == "inner" else 0)
        copy = pltpu.make_async_remote_copy(
            src_ref=source,
            dst_ref=target,
            send_sem=halo_send.at[step, n],
            recv_sem=halo_recv.at[step, n],
            device_id=beside(c),
            device_id_type=MESH,
        )
        copy.start()
        started.setdefault((step, group), []).append(copy)

    def await_halo(step, group):
        for copy in started[step, group]:
            copy.wait_recv()

    def send_x(step, sign):
        side = 0 if sign == 1 else 1
        exit_x = PAD + (BS - 1 if sign == 1 else 0)
        group = ("x", sign)
        for k, i in enumerate(with_component(0, sign)):
            out_x[step, side, k : k + 1, :] = post[step, i, exit_x : exit_x + 1, :]
        for k, i in enumerate(with_component(0, sign)):
            if VELS[i][2]:
                send(step, group, VELS[i], out_x.at[step, side, k : k + 1, :], got_xz.at[step, i - 11])
        send(step, group, (sign, 0, 0), out_x.at[step, side], got_x.at[step, side])
        for k, i in enumerate(with_component(0, sign)):
            cy = VELS[i][1]
            if cy:
                cols = slice(LANES - 128, LANES) if cy == 1 else slice(0, 128)
                send(step, group, VELS[i], out_x.at[step, side, k : k + 1, cols], got_xy.at[step, i - 7])

    def send_yz(step, group, tiles):
        at = 1 if group == "inner" else 0
        begin, end = SPOT[tiles[0]], SPOT[tiles[-1]] + 8
        for i in range(15, 19):
            col = LANES - 128 if VELS[i][1] == 1 else 0
            for t in tiles:
                out_yz[step, at, i - 15, SPOT[t] : SPOT[t] + 8, :] = post[
                    step, i, padded(t), col : col + 128
                ]
            send(
                step,
                group,
                VELS[i],
                out_yz.at[step, at, i - 15, begin:end, :],
                got_yz.at[step, at, i - 15, begin:end, :],
            )
        for side, sign in enumerate((1, -1)):
            exit_z = ROW - 1 if sign == 1 else 0
            packed = None
            for n, t in enumerate(tiles):
                for k, i in enumerate(with_component(2, sign)):
                    q = 3 * (5 * n + k)
                    part = post[step, i, padded(t), :]
                    for g in range(3):
                        turned = pltpu.roll(part, (-sign * (ROW + q + g)) % LANES, 1)
                        piece = turned[:, THIRD * g : THIRD * g + THIRD]
                        if packed is None:
                            packed = piece
                        else:
                            packed = jnp.where(z_third == exit_z - sign * (q + g), piece, packed)
            out_z[step, at, side] = packed
            send(step, group, (0, 0, sign), out_z.at[step, at, side], got_z.at[step, at, side])
        for side, sign in enumerate((1, -1)):
            col = LANES - 128 if sign == 1 else 0
            for k, i in enumerate(with_component(1, sign)):
                for t in tiles:
                    out_y[step, at, side, k, SPOT[t] : SPOT[t] + 8, :] = post[
                        step, i, padded(t), col : col + 128
                    ]
            send(
                step,
                group,
                (0, sign, 0),
                out_y.at[step, at, side, :, begin:end, :],
                got_y.at[step, at, side, :, begin:end, :],
            )

    def fill_yz(step, group, tiles):
        at = 1 if group == "inner" else 0
        tile_lane = lane[:, :128]
        for n, t in enumerate(tiles):
            spot = slice(SPOT[t], SPOT[t] + 8)
            for i in range(3, 19):
                cx, cy, cz = VELS[i]
                if cz:
                    exit_z = ROW - 1 if cz == 1 else 0
                    side = 0 if cz == 1 else 1
                    q = 3 * (5 * n + with_component(2, cz).index(i))
                    packed = got_z[step, at, side]
                    parts = [
                        pltpu.roll(packed, (cz * (q + g)) % THIRD, 1) if q + g else packed
                        for g in range(3)
                    ]
                    post[step, i, padded(t), :] = jnp.where(
                        z == exit_z, jnp.concatenate(parts, axis=1), post[step, i, padded(t), :]
                    )
                if cy:
                    side = 0 if cy == 1 else 1
                    col = LANES - 128 if cy == 1 else 0
                    cols = slice(col, col + 128)
                    leaves = tile_lane >= 128 - ROW if cy == 1 else tile_lane < ROW
                    if cz:
                        leaves = leaves & (z[:, cols] != exit_z)
                    k = with_component(1, cy).index(i)
                    post[step, i, padded(t), cols] = jnp.where(
                        leaves, got_y[step, at, side, k, spot, :], post[step, i, padded(t), cols]
                    )
                if cy and cz:
                    from_y = BS - 1 if cy == 1 else 0
                    slot = ((from_y - cz) % BS) * ROW + exit_z
                    source = from_y * ROW + exit_z
                    cols = slice(slot // 128 * 128, slot // 128 * 128 + 128)
                    edge = pltpu.roll(got_yz[step, at, i - 15, spot, :], (slot - source) % 128, 1)
                    post[step, i, padded(t), cols] = jnp.where(
                        tile_lane == slot % 128, edge, post[step, i, padded(t), cols]
                    )

    def fill_x(step, sign):
        side = 0 if sign == 1 else 1
        row_at = PAD - 1 if sign == 1 else PAD + BS
        one_lane = lane[0:1]
        for k, i in enumerate(with_component(0, sign)):
            cx, cy, cz = VELS[i]
            row = got_x[step, side, k : k + 1, :]
            if cz:
                exit_z = ROW - 1 if cz == 1 else 0
                edge = pltpu.roll(got_xz[step, i - 11], (-cz * ROW) % LANES, 1)
                row = jnp.where(z[0:1] == exit_z, edge, row)
            post[step, i, row_at : row_at + 1, :] = row
            if cy:
                col = LANES - 128 if cy == 1 else 0
                cols = slice(col, col + 128)
                leaves = one_lane[:, :128] >= 128 - ROW if cy == 1 else one_lane[:, :128] < ROW
                post[step, i, row_at : row_at + 1, cols] = jnp.where(
                    leaves, got_xy[step, i - 7], row[:, cols]
                )

    def stream(step, t, which=range(19)):
        target = fields if step == STEPS - 1 else flow
        for i in which:
            cx, cy, cz = VELS[i]
            v = post[step, i, padded(t, -cx), :]
            shift = (cy * ROW + cz) % LANES
            target[i, rows_of(t), :] = pltpu.roll(v, shift, 1) if shift else v

    loads[1].wait()
    pack(0, (18, 0), (18, 1))
    pack_folded(18, 2)
    loads[2].wait()
    pack_tile(0)
    pl.semaphore_wait(barrier, len(partners))
    send_ring(0, slice(0, FIRST_ROW[0] + 9), slice(0, 8))
    send_ring(5, slice(FOLDED, FOLDED + 1), slice(0, 8), slice(0, HALF_COLS))
    loads[3].wait()
    pack_tile(2)
    send_ring(1, slice(FIRST_ROW[2], FIRST_ROW[2] + 9), slice(0, 8))
    loads[4].wait()
    pack_tile(1)
    middle = slice(FIRST_ROW[1], FIRST_ROW[1] + 9)
    send_ring(2, middle, slice(0, 1))
    send_ring(3, middle, slice(7, 8))
    send_ring(4, middle, slice(1, 7))
    loads[5].wait()

    await_ring(0)
    await_ring(5)
    unpack(0, (18, 0), (18, 1))
    unpack_folded(18, 2)
    unpack_tile(0)
    collide_tile(0, 0)
    send_x(0, -1)
    await_ring(1)
    unpack_tile(2)
    collide_tile(0, 2)
    send_x(0, 1)
    await_ring(2)
    await_ring(3)
    unpack_tile(1, slice(0, 1))
    unpack_tile(1, slice(7, 8))
    collide_tile(0, 1)
    send_yz(0, "outer", (0, 2, 1))

    await_ring(4)
    unpack_tile(1)
    collide_tile(0, 1)
    send_yz(0, "inner", (1,))

    await_halo(0, "outer")
    fill_yz(0, "outer", (0, 2, 1))
    await_halo(0, ("x", -1))
    fill_x(0, -1)
    stream(0, 2)
    collide_tile(1, 2)
    send_x(1, 1)
    await_halo(0, ("x", 1))
    fill_x(0, 1)
    stream(0, 0)
    collide_tile(1, 0)
    send_x(1, -1)
    send_yz(1, "outer", (0, 2))

    await_halo(0, "inner")
    fill_yz(0, "inner", (1,))
    stream(0, 1)
    collide_tile(1, 1)
    send_yz(1, "inner", (1,))

    await_halo(1, "outer")
    fill_yz(1, "outer", (0, 2))
    await_halo(1, ("x", 1))
    fill_x(1, 1)
    stream(1, 0, [i for i in range(19) if VELS[i][0] != -1])
    await_halo(1, ("x", -1))
    fill_x(1, -1)
    stream(1, 2, [i for i in range(19) if VELS[i][0] != 1])
    await_halo(1, "inner")
    fill_yz(1, "inner", (1,))
    stream(1, 1)
    stream(1, 0, with_component(0, -1))
    stream(1, 2, with_component(0, 1))
    for copies in list(ring.values()) + list(started.values()):
        for copy in copies:
            copy.wait_send()


def per_device(popul, codes, solid):
    vmem = pl.BlockSpec(memory_space=pltpu.VMEM)
    fields = pl.pallas_call(
        kernel,
        out_shape=jax.ShapeDtypeStruct((19, BS, LANES), jnp.float32),
        in_specs=[pl.BlockSpec(memory_space=pltpu.HBM)] * 3,
        out_specs=vmem,
        scratch_shapes=[
            pltpu.SMEM((2,), jnp.int32),
            pltpu.VMEM((BS, LANES), jnp.int32),
            pltpu.VMEM((19, BS, LANES), jnp.float32),
            pltpu.VMEM((19, BS, LANES), jnp.float32),
            pltpu.VMEM((19, BS, LANES), jnp.float32),
            pltpu.VMEM((STEPS, 19, BS + 2 * PAD, LANES), jnp.float32),
        ]
        + [pltpu.VMEM((PACKED, 8, LANES), jnp.float32)] * 4
        + [
            pltpu.VMEM((STEPS, 2, 5, LANES), jnp.float32),
            pltpu.VMEM((STEPS, 2, 2, 5, BS, 128), jnp.float32),
            pltpu.VMEM((STEPS, 2, 2, 8, THIRD), jnp.float32),
            pltpu.VMEM((STEPS, 2, 4, BS, 128), jnp.float32),
        ]
        * 2
        + [
            pltpu.VMEM((STEPS, 4, 1, 128), jnp.float32),
            pltpu.VMEM((STEPS, 4, 1, LANES), jnp.float32),
            pltpu.SemaphoreType.DMA((6,)),
            pltpu.SemaphoreType.DMA((2, 6)),
            pltpu.SemaphoreType.DMA((2, 6)),
            pltpu.SemaphoreType.DMA((STEPS, 36)),
            pltpu.SemaphoreType.DMA((STEPS, 36)),
        ],
        compiler_params=pltpu.CompilerParams(
            collective_id=0, has_side_effects=True, vmem_limit_bytes=51 * 1024 * 1024
        ),
        cost_estimate=pl.CostEstimate(flops=14_000_000, bytes_accessed=4_500_000, transcendentals=0),
    )(codes, popul.reshape(19, BS, LANES), solid.reshape(BS, LANES))
    return fields.reshape(popul.shape)


def solution(mesh):
    placed = (
        P("gx", "gy", "gz", None, None),
        P(("gx", "gy", "gz")),
        P("gx", "gy", "gz", None, None),
    )
    return jax.shard_map(
        per_device,
        mesh=mesh,
        in_specs=placed,
        out_specs=P("gx", "gy", "gz", None, None),
        check_vma=False,
    )
```
